256 devices in a mesh: docs: 128 (over z, x, y), tiles: 2 (over core).
Axes of the slice: x: 4, y: 4, z: 8, core: 2. Of those that a mesh axis runs over, the one named last changes fastest.
Arguments:
- embeddings: float32 [32768, 1024], P(('docs', 'tiles')), may hold values from -6 to 6
- cluster_of: int32 [32768], P(('docs', 'tiles')), may hold values from 0 to 255, as said below
- row_lists: int32 [256, 512], P('docs'), may hold values from -1 to 511, as said below
- row_counts: int32 [256], P('docs'), may hold values from 0 to 512, as said below
Outputs:
- max_cosine: float32 [32768], P(('docs', 'tiles'))
The draws below stay inside these ranges and needn't reach their ends.
Inputs may be any that keep to these rules, and one draw needn't show every extreme that they name: `cluster_of`: clusters 2 * d to 2 * d + 1 have home d. The documents of one device have at most 2 of one home, and 16 homes receive exactly 2 from every device. `row_lists`: row c lists the places of cluster c's documents in their earlier order and holds -1 from position row_counts[c] on. `row_counts`: some cluster holds 512 documents.
All inputs are finite; a program needn't handle non-finite values.
Results may differ from the reference program's by a relative error of at most 0.0003.
Values sent between devices are 32-bit elements; how exact they have to be, the bound alone decides.
No kernel may reach another device: no remote copies, remote signals or barrier semaphores. Data moves between devices by JAX's collectives and lax.ppermute only.
A program may use at most 64 MiB of HBM per device.

```python
import jax
import jax.numpy as jnp
from jax import lax

D = 1024
TOK_DEV = 128
CL_DEV = 2
TILE = 256
DOCS = 32768
CLUSTERS = 256
SEND_CAP = 2
CAP = 512
HOT = 16
N_DOCS = 128
N_TILES = 2


def place_codes_drawn(cluster_of):
    shards = N_DOCS * N_TILES
    home_rows = (cluster_of // CL_DEV).astype(jnp.int32).reshape(shards, TOK_DEV)

    def slot_ranks(home_row):
        same_home = home_row[:, None] == home_row[None, :]
        earlier = jnp.arange(TOK_DEV, dtype=jnp.int32)[:, None] > jnp.arange(TOK_DEV, dtype=jnp.int32)[None, :]
        return jnp.sum((same_home & earlier).astype(jnp.int32), axis=1).astype(jnp.int32)
    slot_rank = lax.map(slot_ranks, home_rows)
    shard_index = jnp.arange(shards, dtype=jnp.int32)[:, None]
    place_code = shard_index % N_TILES * (N_DOCS * SEND_CAP) + shard_index // N_TILES * SEND_CAP + slot_rank
    return place_code.reshape(-1).astype(jnp.int32)


def layout(key):
    shards = N_DOCS * N_TILES
    slot_total = N_DOCS * SEND_CAP
    key_parts = jax.random.split(key, 5)
    hot_owner = jax.random.permutation(key_parts[0], N_DOCS) < HOT
    slot_home = jnp.arange(slot_total, dtype=jnp.int32) // SEND_CAP
    score_top = (1 << 30) // slot_total
    slot_ids = jnp.arange(slot_total, dtype=jnp.int32)
    scores = jax.random.randint(key_parts[1], (shards, slot_total), 0, score_top, dtype=jnp.int32) * slot_total + slot_ids
    scores = jnp.where(hot_owner[slot_home][None, :], score_top * slot_total + slot_ids, scores)
    chosen = lax.top_k(scores, TOK_DEV)[1].astype(jnp.int32)
    homes = chosen // SEND_CAP
    shuffles = jax.vmap(lambda part_key: jax.random.permutation(part_key, TOK_DEV))(jax.random.split(key_parts[2], shards))
    homes = jnp.take_along_axis(homes, shuffles.astype(jnp.int32), axis=1)
    local_cluster = jax.random.randint(key_parts[3], (shards, TOK_DEV), 0, CL_DEV, dtype=jnp.int32)
    local_cluster = jnp.where(hot_owner[homes], 0, local_cluster)
    cluster = (homes * CL_DEV + local_cluster).reshape(-1).astype(jnp.int32)
    place_code = place_codes_drawn(cluster)
    priority = jax.random.permutation(key_parts[4], DOCS).astype(jnp.int32)
    sort_order = jnp.argsort(cluster * DOCS + priority, stable=True)
    counts = jnp.zeros((CLUSTERS,), jnp.int32).at[cluster].add(1)
    starts = jnp.cumsum(counts) - counts
    sorted_cluster = cluster[sort_order]
    list_place = jnp.arange(DOCS, dtype=jnp.int32) - starts[sorted_cluster]
    lists = jnp.full((CLUSTERS, CAP), -1, jnp.int32).at[sorted_cluster, list_place].set(place_code[sort_order])
    return (cluster, lists, counts)


def draw_cluster_of(key, part):
    return layout(key)[0]


def draw_row_lists(key, part):
    return layout(key)[1]


def draw_row_counts(key, part):
    return layout(key)[2]


def block_scale(stream_key, shape, pieces, smallest, largest):
    def one(position, parts):
        heights = jax.random.uniform(jax.random.fold_in(jax.random.fold_in(stream_key, 6), position), (parts,), jnp.float32, smallest / len(pieces), largest / len(pieces))
        return jnp.repeat(jnp.exp(heights), shape[position] // parts).reshape((-1,) + (1,) * (len(shape) - position - 1))

    factor_of = one(*pieces[0])
    for cut in pieces[1:]:
        factor_of = factor_of * one(*cut)
    return factor_of


def bell_draw(own_key, dims, scale, bound, cuts=(), kind=jnp.bfloat16):
    drawn = scale * jax.random.normal(own_key, dims, jnp.float32)
    if cuts:
        drawn = drawn * block_scale(own_key, dims, cuts, -0.22, 0.18)
    return jnp.clip(drawn, -bound, bound).astype(kind)


def setup_inputs(seed: int = 0) -> dict:
    key_of = jax.random.split(jax.random.key(seed), 5)
    return {
        "embeddings": bell_draw(key_of[0], (DOCS, D), 1.0, 6.0, ((0, 256),), jnp.float32),
        "cluster_of": draw_cluster_of(jax.random.fold_in(key_of[4], 71), 0),
        "row_lists": draw_row_lists(jax.random.fold_in(key_of[4], 71), 0),
        "row_counts": draw_row_counts(jax.random.fold_in(key_of[4], 71), 0),
    }


EPS = 1e-06

def place_codes(cluster_of):
    shards = N_DOCS * N_TILES
    home_rows = (cluster_of // CL_DEV).astype(jnp.int32).reshape(shards, TOK_DEV)

    def slot_ranks(home_row):
        same_home = home_row[:, None] == home_row[None, :]
        earlier = jnp.arange(TOK_DEV, dtype=jnp.int32)[:, None] > jnp.arange(TOK_DEV, dtype=jnp.int32)[None, :]
        return lax.optimization_barrier(jnp.sum((same_home & earlier).astype(jnp.int32), axis=1)).astype(jnp.int32)
    slot_rank = lax.map(slot_ranks, home_rows)
    shard_index = jnp.arange(shards, dtype=jnp.int32)[:, None]
    place_code = shard_index % N_TILES * (N_DOCS * SEND_CAP) + shard_index // N_TILES * SEND_CAP + slot_rank
    return (home_rows.reshape(-1), place_code.reshape(-1).astype(jnp.int32))

def reference(embeddings, cluster_of, row_lists, row_counts):
    home_index, place_code = place_codes(cluster_of)
    buffer_rows = N_TILES * N_DOCS * SEND_CAP
    doc_of = jnp.zeros((N_DOCS * buffer_rows,), jnp.int32).at[home_index * buffer_rows + place_code].set(jnp.arange(DOCS, dtype=jnp.int32))
    unit_rows = embeddings * lax.rsqrt(lax.optimization_barrier(jnp.sum(embeddings * embeddings, axis=1, keepdims=True)) + EPS)

    def one_cluster(packed):
        list_row, list_count, cluster_home = packed
        doc_index = doc_of[cluster_home * buffer_rows + jnp.maximum(list_row, 0)]
        cluster_rows = unit_rows[doc_index]
        tile_count = (list_count + TILE - 1) // TILE

        def outer_step(row_tile, maxima):
            query_rows = lax.dynamic_slice_in_dim(cluster_rows, row_tile * TILE, TILE, 0)
            query_pos = row_tile * TILE + jnp.arange(TILE, dtype=jnp.int32)

            def inner_step(col_tile, best_score):
                key_rows = lax.dynamic_slice_in_dim(cluster_rows, col_tile * TILE, TILE, 0)
                scores = jnp.einsum('qd,kd->qk', query_rows, key_rows, precision=lax.Precision.HIGHEST, preferred_element_type=jnp.float32)
                key_pos = col_tile * TILE + jnp.arange(TILE, dtype=jnp.int32)
                masked = jnp.where(key_pos[None, :] < query_pos[:, None], scores, -1.0)
                return jnp.maximum(best_score, lax.optimization_barrier(jnp.max(masked, axis=1)))
            best_score = lax.fori_loop(0, row_tile + 1, inner_step, jnp.full((TILE,), -1.0, jnp.float32))
            return lax.dynamic_update_slice_in_dim(maxima, best_score, row_tile * TILE, 0)
        maxima = lax.fori_loop(0, tile_count, outer_step, jnp.full((CAP,), -1.0, jnp.float32))
        target = jnp.where(jnp.arange(CAP, dtype=jnp.int32) < list_count, doc_index, DOCS)
        return (maxima, target)
    cluster_homes = jnp.arange(CLUSTERS, dtype=jnp.int32) // CL_DEV
    maxima, target = lax.map(one_cluster, (row_lists, row_counts, cluster_homes))
    return jnp.full((DOCS,), -1.0, jnp.float32).at[target.reshape(-1)].set(maxima.reshape(-1), mode='drop')
```

```python
import functools

import jax
import jax.numpy as jnp
from jax import lax
from jax.experimental import pallas as pl
from jax.experimental.pallas import tpu as pltpu
from jax.sharding import PartitionSpec as P

EPS = 1e-06
LANES = 128
PARAMS = pltpu.CompilerParams(vmem_limit_bytes=32 * 1024 * 1024)


def parts_of(rows):
    high = rows.astype(jnp.bfloat16)
    rest = rows - high.astype(jnp.float32)
    return high, rest


def prep_kernel(cl_local, send_cap, cluster_ref, rows_ref, out_ref, slot_ref):
    docs, width = rows_ref.shape
    slots = out_ref.shape[0] * LANES // width
    chunks = width // LANES
    home = lax.shift_right_logical(cluster_ref[...], cl_local.bit_length() - 1)
    across = jnp.broadcast_to(home, (docs, docs))
    down = across.T
    sub = lax.broadcasted_iota(jnp.int32, (docs, docs), 0)
    lane = lax.broadcasted_iota(jnp.int32, (docs, docs), 1)
    before = jnp.where((across == down) & (sub < lane), 1, 0)
    slot = home * send_cap + jnp.sum(before, axis=0, keepdims=True)
    slot_ref[...] = slot
    place = lax.broadcasted_iota(jnp.int32, (slots, docs), 0)
    chosen = jnp.where(place == slot, 1.0, 0.0).astype(jnp.bfloat16)
    rows = rows_ref[...]
    unit = rows * lax.rsqrt(jnp.sum(rows * rows, axis=1, keepdims=True) + EPS)
    high, rest = parts_of(unit)
    middle, rest = parts_of(rest)
    low = rest.astype(jnp.bfloat16)

    def put(part):
        return jnp.dot(chosen, part, preferred_element_type=jnp.float32)

    placed = put(high) + put(middle) + put(low)
    for chunk in range(chunks):
        out_ref[pl.ds(chunk, slots, stride=chunks), :] = placed[
            :, chunk * LANES : (chunk + 1) * LANES
        ]


def split_rows(rows_ref, high_ref, low_ref, send_cap):
    count, width = high_ref.shape
    chunks = width // LANES
    each = count // send_cap
    for rank in range(send_cap):
        for chunk in range(chunks):
            part = rows_ref[pl.ds(rank * chunks + chunk, each, stride=send_cap * chunks), :]
            high, rest = parts_of(part)
            cols = slice(chunk * LANES, (chunk + 1) * LANES)
            high_ref[rank * each : (rank + 1) * each, cols] = high
            low_ref[rank * each : (rank + 1) * each, cols] = rest.astype(jnp.bfloat16)


def codes_of(lists, counts, half, rows, send_cap):
    cap = lists.shape[1]
    each = rows // send_cap
    row = lax.broadcasted_iota(jnp.int32, (rows, 1), 0)
    rank = row // each
    place = half * rows + (row - rank * each) * send_cap + rank
    position = lax.broadcasted_iota(jnp.int32, (1, cap), 1)
    code = jnp.full((rows, cap), -1, jnp.int32)
    for cluster in range(lists.shape[0]):
        listed = jnp.where(position < counts[cluster], lists[cluster : cluster + 1, :], -1)
        code = jnp.where(listed == place, position + cluster * cap, code)
    return jnp.max(code, axis=1, keepdims=True)


def across_lanes(column):
    wide = jnp.broadcast_to(column, (column.shape[0], LANES))
    return wide.T[:1, :]


def nt(left, right):
    return lax.dot_general(
        left, right, (((1,), (1,)), ((), ())), preferred_element_type=jnp.float32
    )


def best_of(q_high, q_low, k_high, k_low, q_code, k_code, cap):
    scores = nt(q_high, k_high) + (nt(q_high, k_low) + nt(q_low, k_high))
    first = q_code // cap * cap
    allowed = (k_code < q_code) & (k_code >= first)
    return jnp.max(jnp.where(allowed, scores, -1.0), axis=1, keepdims=True)


def gram_kernel(send_cap, lists_ref, counts_ref, core_ref, own_ref, other_ref, out_ref,
                own_high, own_low, other_high, other_low):
    rows = own_high.shape[0]
    each = rows // send_cap
    cap = lists_ref.shape[1]
    lists = lists_ref[...]
    counts = [counts_ref[index] for index in range(lists.shape[0])]
    core = core_ref[0]
    own_code = codes_of(lists, counts, core, rows, send_cap)
    other_code = codes_of(lists, counts, 1 - core, rows, send_cap)
    split_rows(own_ref, own_high, own_low, send_cap)
    split_rows(other_ref, other_high, other_low, send_cap)
    q_high, q_low = own_high[...], own_low[...]
    best = best_of(q_high, q_low, q_high, q_low, own_code, across_lanes(own_code), cap)
    best = jnp.maximum(
        best,
        best_of(q_high, q_low, other_high[...], other_low[...], own_code,
                across_lanes(other_code), cap),
    )
    lane = lax.broadcasted_iota(jnp.int32, (each, LANES), 1)
    out = jnp.broadcast_to(best[:each], (each, LANES))
    for rank in range(1, send_cap):
        out = jnp.where(lane == rank, best[rank * each : (rank + 1) * each], out)
    out_ref[...] = out


def pick_kernel(send_cap, slot_ref, back_ref, out_ref):
    homes = back_ref.shape[0]
    docs = slot_ref.shape[1]
    slot = slot_ref[...]
    home = lax.broadcasted_iota(jnp.int32, (homes, docs), 0)
    back = back_ref[...]
    picked = jnp.zeros((homes, docs), jnp.float32)
    for rank in range(send_cap):
        value = jnp.broadcast_to(back[:, rank : rank + 1], (homes, docs))
        picked = jnp.where(slot == home * send_cap + rank, value, picked)
    out_ref[...] = jnp.sum(picked, axis=0, keepdims=True)


def local(embeddings, cluster_of, row_lists, row_counts):
    n_docs = lax.axis_size("docs")
    n_tiles = lax.axis_size("tiles")
    doc_count, width = embeddings.shape
    send_cap = n_tiles * doc_count // n_docs
    cl_local = row_lists.shape[0]
    core = lax.axis_index("tiles").astype(jnp.int32).reshape(1)
    slots = n_docs * send_cap
    flat = (slots * width // LANES, LANES)
    vmem = pl.BlockSpec(memory_space=pltpu.VMEM)
    smem = pl.BlockSpec(memory_space=pltpu.SMEM)

    outgoing, slot = pl.pallas_call(
        functools.partial(prep_kernel, cl_local, send_cap),
        out_shape=(
            jax.ShapeDtypeStruct(flat, jnp.float32),
            jax.ShapeDtypeStruct((1, doc_count), jnp.int32),
        ),
        in_specs=[vmem, vmem],
        out_specs=(vmem, vmem),
        compiler_params=PARAMS,
        name="prep",
    )(cluster_of.reshape(1, doc_count), embeddings)

    def exchange(blocks):
        return lax.all_to_all(blocks, "docs", split_axis=0, concat_axis=0, tiled=True)

    own = exchange(outgoing.reshape(n_docs, -1, LANES)).reshape(flat)
    other = lax.ppermute(own, "tiles", [(0, 1), (1, 0)])

    half = pltpu.VMEM((slots, width), jnp.bfloat16)
    best = pl.pallas_call(
        functools.partial(gram_kernel, send_cap),
        out_shape=jax.ShapeDtypeStruct((n_docs, LANES), jnp.float32),
        in_specs=[vmem, smem, smem, vmem, vmem],
        out_specs=vmem,
        scratch_shapes=[half, half, half, half],
        compiler_params=PARAMS,
        name="gram",
    )(row_lists, row_counts, core, own, other)

    back = exchange(best.reshape(n_docs, 1, LANES)).reshape(n_docs, LANES)
    picked = pl.pallas_call(
        functools.partial(pick_kernel, send_cap),
        out_shape=jax.ShapeDtypeStruct((1, doc_count), jnp.float32),
        in_specs=[vmem, vmem],
        out_specs=vmem,
        compiler_params=PARAMS,
        name="pick",
    )(slot, back)
    return picked.reshape(doc_count)


def solution(mesh):
    placed = (P(("docs", "tiles"), None), P(("docs", "tiles")), P("docs", None), P("docs"))
    return jax.shard_map(
        local, mesh=mesh, in_specs=placed, out_specs=P(("docs", "tiles")), check_vma=False
    )
```

```python
import functools

import jax
import jax.numpy as jnp
from jax import lax
from jax.experimental import pallas as pl
from jax.experimental.pallas import tpu as pltpu
from jax.sharding import PartitionSpec as P

EPS = 1e-06
LANES = 128
PIECES = 4
FIRST = 74
PARAMS = pltpu.CompilerParams(vmem_limit_bytes=32 * 1024 * 1024)


def regroup(index):
    return index ^ FIRST


def parts_of(rows):
    high = rows.astype(jnp.bfloat16)
    rest = rows - high.astype(jnp.float32)
    return high, rest


def prep_kernel(cl_local, send_cap, cluster_hbm, rows_hbm, out_ref, slot_ref,
                cluster_ref, rows_ref, cluster_sem, rows_sems):
    docs, width = rows_ref.shape
    slots = out_ref.shape[0] * LANES // width
    chunks = width // LANES
    pieces = rows_sems.shape[0]
    piece = docs // pieces
    cluster_copy = pltpu.make_async_copy(cluster_hbm, cluster_ref, cluster_sem)
    cluster_copy.start()
    copies = []
    for index in range(pieces):
        span = pl.ds(index * piece, piece)
        copies.append(
            pltpu.make_async_copy(rows_hbm.at[span], rows_ref.at[span], rows_sems.at[index])
        )
        copies[-1].start()
    cluster_copy.wait()
    home = lax.shift_right_logical(cluster_ref[...], cl_local.bit_length() - 1)
    across = jnp.broadcast_to(home, (docs, docs))
    down = across.T
    sub = lax.broadcasted_iota(jnp.int32, (docs, docs), 0)
    lane = lax.broadcasted_iota(jnp.int32, (docs, docs), 1)
    before = jnp.where((across == down) & (sub < lane), 1, 0)
    slot = regroup(home) * send_cap + jnp.sum(before, axis=0, keepdims=True)
    slot_ref[...] = slot
    place = lax.broadcasted_iota(jnp.int32, (slots, docs), 0)
    chosen = jnp.where(place == slot, 1.0, 0.0).astype(jnp.bfloat16)
    units = []
    for index in range(pieces):
        copies[index].wait()
        rows = rows_ref[index * piece : (index + 1) * piece, :]
        units.append(rows * lax.rsqrt(jnp.sum(rows * rows, axis=1, keepdims=True) + EPS))
    high, rest = parts_of(jnp.concatenate(units, axis=0))
    middle, rest = parts_of(rest)
    low = rest.astype(jnp.bfloat16)

    def put(part):
        return jnp.dot(chosen, part, preferred_element_type=jnp.float32)

    placed = put(high) + put(middle) + put(low)
    for chunk in range(chunks):
        out_ref[pl.ds(chunk, slots, stride=chunks), :] = placed[
            :, chunk * LANES : (chunk + 1) * LANES
        ]


def split_rows(rows_ref, high_ref, low_ref, send_cap):
    count, width = high_ref.shape
    chunks = width // LANES
    each = count // send_cap
    for rank in range(send_cap):
        for chunk in range(chunks):
            part = rows_ref[pl.ds(rank * chunks + chunk, each, stride=send_cap * chunks), :]
            high, rest = parts_of(part)
            cols = slice(chunk * LANES, (chunk + 1) * LANES)
            high_ref[rank * each : (rank + 1) * each, cols] = high
            low_ref[rank * each : (rank + 1) * each, cols] = rest.astype(jnp.bfloat16)


def codes_of(lists, counts, half, rows, send_cap):
    cap = lists.shape[1]
    each = rows // send_cap
    row = lax.broadcasted_iota(jnp.int32, (rows, 1), 0)
    rank = row // each
    place = half * rows + regroup(row - rank * each) * send_cap + rank
    position = lax.broadcasted_iota(jnp.int32, (1, cap), 1)
    code = jnp.full((rows, cap), -1, jnp.int32)
    for cluster in range(lists.shape[0]):
        listed = jnp.where(position < counts[cluster], lists[cluster : cluster + 1, :], -1)
        code = jnp.where(listed == place, position + cluster * cap, code)
    return jnp.max(code, axis=1, keepdims=True)


def across_lanes(column):
    wide = jnp.broadcast_to(column, (column.shape[0], LANES))
    return wide.T[:1, :]


def nt(left, right):
    return lax.dot_general(
        left, right, (((1,), (1,)), ((), ())), preferred_element_type=jnp.float32
    )


def best_of(q_high, q_low, k_high, k_low, q_code, k_code, cap):
    scores = nt(q_high, k_high) + (nt(q_high, k_low) + nt(q_low, k_high))
    first = q_code // cap * cap
    allowed = (k_code < q_code) & (k_code >= first)
    return jnp.max(jnp.where(allowed, scores, -1.0), axis=1, keepdims=True)


def near_kernel(send_cap, lists_ref, counts_ref, core_ref, own_ref,
                high_ref, low_ref, own_code_ref, other_code_ref, best_ref):
    rows = high_ref.shape[0]
    cap = lists_ref.shape[1]
    lists = lists_ref[...]
    counts = [counts_ref[index] for index in range(lists.shape[0])]
    core = core_ref[0]
    own_code = codes_of(lists, counts, core, rows, send_cap)
    own_code_ref[...] = own_code
    other_code_ref[...] = across_lanes(codes_of(lists, counts, 1 - core, rows, send_cap))
    split_rows(own_ref, high_ref, low_ref, send_cap)
    high, low = high_ref[...], low_ref[...]
    best_ref[...] = best_of(high, low, high, low, own_code, across_lanes(own_code), cap)


def far_kernel(send_cap, cap, high_ref, low_ref, own_code_ref, other_code_ref, best_ref,
               other_ref, out_ref, other_high, other_low):
    rows = high_ref.shape[0]
    each = rows // send_cap
    split_rows(other_ref, other_high, other_low, send_cap)
    best = jnp.maximum(
        best_ref[...],
        best_of(high_ref[...], low_ref[...], other_high[...], other_low[...],
                own_code_ref[...], other_code_ref[...], cap),
    )
    lane = lax.broadcasted_iota(jnp.int32, (each, LANES), 1)
    out = jnp.broadcast_to(best[:each], (each, LANES))
    for rank in range(1, send_cap):
        out = jnp.where(lane == rank, best[rank * each : (rank + 1) * each], out)
    out_ref[...] = out


def pick_kernel(send_cap, slot_ref, back_ref, out_ref):
    homes = back_ref.shape[0]
    docs = slot_ref.shape[1]
    slot = slot_ref[...]
    home = lax.broadcasted_iota(jnp.int32, (homes, docs), 0)
    back = back_ref[...]
    picked = jnp.zeros((homes, docs), jnp.float32)
    for rank in range(send_cap):
        value = jnp.broadcast_to(back[:, rank : rank + 1], (homes, docs))
        picked = jnp.where(slot == home * send_cap + rank, value, picked)
    out_ref[...] = jnp.sum(picked, axis=0, keepdims=True)


def local(embeddings, cluster_of, row_lists, row_counts):
    n_docs = lax.axis_size("docs")
    n_tiles = lax.axis_size("tiles")
    doc_count, width = embeddings.shape
    send_cap = n_tiles * doc_count // n_docs
    cl_local = row_lists.shape[0]
    core = lax.axis_index("tiles").astype(jnp.int32).reshape(1)
    slots = n_docs * send_cap
    flat = (slots * width // LANES, LANES)
    vmem = pl.BlockSpec(memory_space=pltpu.VMEM)
    smem = pl.BlockSpec(memory_space=pltpu.SMEM)

    hbm = pl.BlockSpec(memory_space=pltpu.HBM)

    def in_hbm(array):
        return pltpu.with_memory_space_constraint(array, pltpu.HBM)

    outgoing, slot = pl.pallas_call(
        functools.partial(prep_kernel, cl_local, send_cap),
        out_shape=(
            jax.ShapeDtypeStruct(flat, jnp.float32),
            jax.ShapeDtypeStruct((1, doc_count), jnp.int32),
        ),
        in_specs=[hbm, hbm],
        out_specs=(vmem, vmem),
        scratch_shapes=[
            pltpu.VMEM((1, doc_count), jnp.int32),
            pltpu.VMEM((doc_count, width), jnp.float32),
            pltpu.SemaphoreType.DMA,
            pltpu.SemaphoreType.DMA((PIECES,)),
        ],
        compiler_params=PARAMS,
        name="prep",
    )(in_hbm(cluster_of.reshape(1, doc_count)), in_hbm(embeddings))

    def exchange(blocks):
        return lax.all_to_all(
            blocks, "docs", split_axis=0, concat_axis=0, tiled=True,
            axis_index_groups=[[regroup(index) for index in range(n_docs)]],
        )

    own = exchange(outgoing.reshape(n_docs, -1, LANES)).reshape(flat)
    other = lax.ppermute(own, "tiles", [(0, 1), (1, 0)])

    half = jax.ShapeDtypeStruct((slots, width), jnp.bfloat16)
    near = pl.pallas_call(
        functools.partial(near_kernel, send_cap),
        out_shape=(
            half,
            half,
            jax.ShapeDtypeStruct((slots, 1), jnp.int32),
            jax.ShapeDtypeStruct((1, slots), jnp.int32),
            jax.ShapeDtypeStruct((slots, 1), jnp.float32),
        ),
        in_specs=[vmem, smem, smem, vmem],
        out_specs=(vmem,) * 5,
        compiler_params=PARAMS,
        name="near",
    )(row_lists, row_counts, core, own)
    best = pl.pallas_call(
        functools.partial(far_kernel, send_cap, row_lists.shape[1]),
        out_shape=jax.ShapeDtypeStruct((n_docs, LANES), jnp.float32),
        in_specs=[vmem] * 6,
        out_specs=vmem,
        scratch_shapes=[pltpu.VMEM((slots, width), jnp.bfloat16)] * 2,
        compiler_params=PARAMS,
        name="far",
    )(*near, other)

    back = exchange(best.reshape(n_docs, 1, LANES)).reshape(n_docs, LANES)
    picked = pl.pallas_call(
        functools.partial(pick_kernel, send_cap),
        out_shape=jax.ShapeDtypeStruct((1, doc_count), jnp.float32),
        in_specs=[vmem, vmem],
        out_specs=vmem,
        compiler_params=PARAMS,
        name="pick",
    )(slot, back)
    return picked.reshape(doc_count)


def solution(mesh):
    placed = (P(("docs", "tiles"), None), P(("docs", "tiles")), P("docs", None), P("docs"))
    return jax.shard_map(
        local, mesh=mesh, in_specs=placed, out_specs=P(("docs", "tiles")), check_vma=False
    )
```

```python
import functools

import jax
import jax.numpy as jnp
from jax import lax
from jax.experimental import pallas as pl
from jax.experimental.pallas import tpu as pltpu
from jax.sharding import PartitionSpec as P

EPS = 1e-06
LANES = 128
FIRST = 74
PARAMS = pltpu.CompilerParams(vmem_limit_bytes=32 * 1024 * 1024)


def regroup(index):
    return index ^ FIRST


def parts_of(rows):
    high = rows.astype(jnp.bfloat16)
    rest = rows - high.astype(jnp.float32)
    return high, rest


def codes_of(lists, counts, half, rows, send_cap):
    cap = lists.shape[1]
    each = rows // send_cap
    row = lax.broadcasted_iota(jnp.int32, (rows, 1), 0)
    rank = row // each
    place = half * rows + regroup(row - rank * each) * send_cap + rank
    position = lax.broadcasted_iota(jnp.int32, (1, cap), 1)
    code = jnp.full((rows, cap), -1, jnp.int32)
    for cluster in range(lists.shape[0]):
        listed = jnp.where(position < counts[:, cluster : cluster + 1],
                           lists[cluster : cluster + 1, :], -1)
        code = jnp.where(listed == place, position + cluster * cap, code)
    return jnp.max(code, axis=1, keepdims=True)


def prep_kernel(cl_local, send_cap, cluster_hbm, lists_hbm, counts_hbm, rows_hbm,
                out_ref, slot_ref, lists_ref, counts_ref, cluster_ref, rows_ref, sems):
    docs, width = rows_ref.shape
    slots = out_ref.shape[0] * LANES // width
    chunks = width // LANES
    copies = [
        pltpu.make_async_copy(source, target, sems.at[index])
        for index, (source, target) in enumerate(
            (
                (cluster_hbm, cluster_ref),
                (lists_hbm, lists_ref),
                (counts_hbm, counts_ref),
                (rows_hbm, rows_ref),
            )
        )
    ]
    for copy in copies:
        copy.start()
    copies[0].wait()
    home = lax.shift_right_logical(cluster_ref[...], cl_local.bit_length() - 1)
    across = jnp.broadcast_to(home, (docs, docs))
    down = across.T
    sub = lax.broadcasted_iota(jnp.int32, (docs, docs), 0)
    lane = lax.broadcasted_iota(jnp.int32, (docs, docs), 1)
    before = jnp.where((across == down) & (sub < lane), 1, 0)
    slot = regroup(home) * send_cap + jnp.sum(before, axis=0, keepdims=True)
    slot_ref[...] = slot
    place = lax.broadcasted_iota(jnp.int32, (slots, docs), 0)
    chosen = jnp.where(place == slot, 1.0, 0.0).astype(jnp.bfloat16)
    copies[-1].wait()
    rows = rows_ref[...]
    unit = rows * lax.rsqrt(jnp.sum(rows * rows, axis=1, keepdims=True) + EPS)
    high, rest = parts_of(unit)
    placed = jnp.dot(
        jnp.concatenate([chosen, chosen], axis=1),
        jnp.concatenate([high, rest.astype(jnp.bfloat16)], axis=0),
        preferred_element_type=jnp.float32,
    )
    for chunk in range(chunks):
        out_ref[pl.ds(chunk, slots, stride=chunks), :] = placed[
            :, chunk * LANES : (chunk + 1) * LANES
        ]
    for copy in copies[1:-1]:
        copy.wait()


def split_rows(rows_ref, high_ref, low_ref, send_cap):
    count, width = high_ref.shape
    chunks = width // LANES
    each = count // send_cap
    for rank in range(send_cap):
        for chunk in range(chunks):
            part = rows_ref[pl.ds(rank * chunks + chunk, each, stride=send_cap * chunks), :]
            high, rest = parts_of(part)
            cols = slice(chunk * LANES, (chunk + 1) * LANES)
            high_ref[rank * each : (rank + 1) * each, cols] = high
            low_ref[rank * each : (rank + 1) * each, cols] = rest.astype(jnp.bfloat16)


def across_lanes(column):
    wide = jnp.broadcast_to(column, (column.shape[0], LANES))
    return wide.T[:1, :]


def masked_max(scores, key_code, query_code, cap):
    first = query_code // cap * cap
    allowed = (key_code < query_code) & (key_code >= first)
    return jnp.max(jnp.where(allowed, scores, -1.0), axis=0, keepdims=True)


def best_of(key_high, key_low, high_turned, low_turned, key_code, query_code, cap):
    def dot(keys, queries):
        return jnp.dot(keys, queries, preferred_element_type=jnp.float32)

    scores = dot(key_high, high_turned) + (
        dot(key_high, low_turned) + dot(key_low, high_turned)
    )
    return masked_max(scores, key_code, query_code, cap)


def near_kernel(send_cap, lists_ref, counts_ref, own_ref, high_ref, low_ref, best_ref,
                other_code_ref, query_code_ref, own_high, own_low):
    slots = own_high.shape[0]
    cap = lists_ref.shape[1]
    core = lax.axis_index("tiles").astype(jnp.int32)
    lists, counts = lists_ref[...], counts_ref[...]
    own_code = codes_of(lists, counts, core, slots, send_cap)
    query_code = across_lanes(own_code)
    query_code_ref[...] = query_code
    other_code_ref[...] = codes_of(lists, counts, 1 - core, slots, send_cap)
    split_rows(own_ref, own_high, own_low, send_cap)
    high, low = own_high[...], own_low[...]
    high_ref[...] = high.T
    low_ref[...] = low.T
    best_ref[...] = best_of(
        high, low, high_ref[...], low_ref[...], own_code, query_code, cap
    )


def far_kernel(send_cap, cap, high_ref, low_ref, best_ref, other_code_ref, query_code_ref,
               other_ref, out_ref):
    width, rows = high_ref.shape
    each = rows // send_cap
    chunks = width // LANES
    step = 2
    scores = jnp.zeros((rows, rows), jnp.float32)
    for begin in range(0, chunks, step):
        part = jnp.concatenate(
            [
                jnp.concatenate(
                    [
                        other_ref[pl.ds(rank * chunks + chunk, each, stride=send_cap * chunks), :]
                        for rank in range(send_cap)
                    ],
                    axis=0,
                )
                for chunk in range(begin, begin + step)
            ],
            axis=1,
        )
        high, rest = parts_of(part)
        low = rest.astype(jnp.bfloat16)
        span = slice(begin * LANES, (begin + step) * LANES)
        high_turned, low_turned = high_ref[span, :], low_ref[span, :]
        scores += (
            jnp.dot(high, high_turned, preferred_element_type=jnp.float32)
            + jnp.dot(high, low_turned, preferred_element_type=jnp.float32)
            + jnp.dot(low, high_turned, preferred_element_type=jnp.float32)
        )
    best = jnp.maximum(
        best_ref[...], masked_max(scores, other_code_ref[...], query_code_ref[...], cap)
    )
    lane = lax.broadcasted_iota(jnp.int32, (each, LANES), 1)
    out = jnp.zeros((each, LANES), jnp.float32)
    for rank in range(send_cap):
        column = jnp.broadcast_to(best[:, rank * each : (rank + 1) * each], (LANES, each)).T
        out = jnp.where(lane == rank, column, out)
    out_ref[...] = out


def pick_kernel(send_cap, slot_ref, back_ref, out_ref):
    homes = back_ref.shape[0]
    docs = slot_ref.shape[1]
    slot = slot_ref[...]
    home = lax.broadcasted_iota(jnp.int32, (homes, docs), 0)
    back = back_ref[...]
    picked = jnp.zeros((homes, docs), jnp.float32)
    for rank in range(send_cap):
        value = jnp.broadcast_to(back[:, rank : rank + 1], (homes, docs))
        picked = jnp.where(slot == home * send_cap + rank, value, picked)
    out_ref[...] = jnp.sum(picked, axis=0, keepdims=True)


def local(embeddings, cluster_of, row_lists, row_counts):
    n_docs = lax.axis_size("docs")
    n_tiles = lax.axis_size("tiles")
    doc_count, width = embeddings.shape
    send_cap = n_tiles * doc_count // n_docs
    cl_local = row_lists.shape[0]
    slots = n_docs * send_cap
    flat = (slots * width // LANES, LANES)
    vmem = pl.BlockSpec(memory_space=pltpu.VMEM)

    hbm = pl.BlockSpec(memory_space=pltpu.HBM)

    def in_hbm(array):
        return pltpu.with_memory_space_constraint(array, pltpu.HBM)

    outgoing, slot, lists, counts = pl.pallas_call(
        functools.partial(prep_kernel, cl_local, send_cap),
        out_shape=(
            jax.ShapeDtypeStruct(flat, jnp.float32),
            jax.ShapeDtypeStruct((1, doc_count), jnp.int32),
            jax.ShapeDtypeStruct(row_lists.shape, jnp.int32),
            jax.ShapeDtypeStruct((1, cl_local), jnp.int32),
        ),
        in_specs=[hbm] * 4,
        out_specs=(vmem,) * 4,
        scratch_shapes=[
            pltpu.VMEM((1, doc_count), jnp.int32),
            pltpu.VMEM((doc_count, width), jnp.float32),
            pltpu.SemaphoreType.DMA((4,)),
        ],
        compiler_params=PARAMS,
        name="prep",
    )(
        in_hbm(cluster_of.reshape(1, doc_count)),
        in_hbm(row_lists),
        in_hbm(row_counts.reshape(1, cl_local)),
        in_hbm(embeddings),
    )

    def exchange(blocks):
        return lax.all_to_all(
            blocks, "docs", split_axis=0, concat_axis=0, tiled=True,
            axis_index_groups=[[regroup(index) for index in range(n_docs)]],
        )

    own = exchange(outgoing.reshape(n_docs, -1, LANES)).reshape(flat)
    other = lax.ppermute(own, "tiles", [(0, 1), (1, 0)])

    cap = row_lists.shape[1]
    turned = jax.ShapeDtypeStruct((width, slots), jnp.bfloat16)
    parts = [pltpu.VMEM((slots, width), jnp.bfloat16)] * 2
    near = pl.pallas_call(
        functools.partial(near_kernel, send_cap),
        out_shape=(
            turned,
            turned,
            jax.ShapeDtypeStruct((1, slots), jnp.float32),
            jax.ShapeDtypeStruct((slots, 1), jnp.int32),
            jax.ShapeDtypeStruct((1, slots), jnp.int32),
        ),
        in_specs=[vmem] * 3,
        out_specs=(vmem,) * 5,
        scratch_shapes=parts,
        compiler_params=PARAMS,
        name="near",
    )(lists, counts, own)
    best = pl.pallas_call(
        functools.partial(far_kernel, send_cap, cap),
        out_shape=jax.ShapeDtypeStruct((n_docs, LANES), jnp.float32),
        in_specs=[vmem] * 6,
        out_specs=vmem,
        compiler_params=PARAMS,
        name="far",
    )(*near, other)

    back = exchange(best.reshape(n_docs, 1, LANES)).reshape(n_docs, LANES)
    picked = pl.pallas_call(
        functools.partial(pick_kernel, send_cap),
        out_shape=jax.ShapeDtypeStruct((1, doc_count), jnp.float32),
        in_specs=[vmem, vmem],
        out_specs=vmem,
        compiler_params=PARAMS,
        name="pick",
    )(slot, back)
    return picked.reshape(doc_count)


def solution(mesh):
    placed = (P(("docs", "tiles"), None), P(("docs", "tiles")), P("docs", None), P("docs"))
    return jax.shard_map(
        local, mesh=mesh, in_specs=placed, out_specs=P(("docs", "tiles")), check_vma=False
    )
```

```python
import functools

import jax
import jax.numpy as jnp
import numpy as np
from jax import lax
from jax.experimental import pallas as pl
from jax.experimental.pallas import tpu as pltpu
from jax.sharding import PartitionSpec as P

EPS = 1e-06
LANES = 128
GRID = (8, 4, 4)
PARAMS = pltpu.CompilerParams(vmem_limit_bytes=32 * 1024 * 1024)


def group_order():
    spots = [
        (z, x, y) for z in range(GRID[0]) for x in range(GRID[1]) for y in range(GRID[2])
    ]

    def distance(spot):
        gaps = [abs(at - size // 2) for at, size in zip(spot, GRID)]
        return sum(min(gap, size - gap) for gap, size in zip(gaps, GRID))

    return sorted(
        range(len(spots)), key=lambda index: (distance(spots[index]) > 0, -distance(spots[index]))
    )


def parts_of(rows):
    high = rows.astype(jnp.bfloat16)
    rest = rows - high.astype(jnp.float32)
    return high, rest


def codes_of(lists, counts, half, key):
    cap = lists.shape[1]
    rows = key.shape[0]
    place = half * rows + key
    position = lax.broadcasted_iota(jnp.int32, (1, cap), 1)
    code = jnp.full((rows, cap), -1, jnp.int32)
    for cluster in range(lists.shape[0]):
        listed = jnp.where(position < counts[:, cluster : cluster + 1],
                           lists[cluster : cluster + 1, :], -1)
        code = jnp.where(listed == place, position + cluster * cap, code)
    return jnp.max(code, axis=1, keepdims=True)


def prep_kernel(cl_local, send_cap, table_hbm, cluster_hbm, lists_hbm, counts_hbm, rows_hbm,
                out_ref, slot_ref, table_ref, lists_ref, counts_ref,
                cluster_ref, rows_ref, sems):
    docs, width = rows_ref.shape
    slots = out_ref.shape[0] * LANES // width
    chunks = width // LANES
    copies = [
        pltpu.make_async_copy(source, target, sems.at[index])
        for index, (source, target) in enumerate(
            (
                (cluster_hbm, cluster_ref),
                (table_hbm, table_ref),
                (lists_hbm, lists_ref),
                (counts_hbm, counts_ref),
                (rows_hbm, rows_ref),
            )
        )
    ]
    for copy in copies:
        copy.start()
    for copy in copies[:2]:
        copy.wait()
    home = lax.shift_right_logical(cluster_ref[...], cl_local.bit_length() - 1)
    across = jnp.broadcast_to(home, (docs, docs))
    down = across.T
    sub = lax.broadcasted_iota(jnp.int32, (docs, docs), 0)
    lane = lax.broadcasted_iota(jnp.int32, (docs, docs), 1)
    before = jnp.where((across == down) & (sub < lane), 1, 0)
    rank = jnp.sum(before, axis=0, keepdims=True)
    slot_ref[...] = home * send_cap + rank
    homes = slots // send_cap
    named = lax.broadcasted_iota(jnp.int32, (homes, docs), 0) == home
    blocks = jnp.broadcast_to(table_ref[1:, :homes].astype(jnp.float32), (8, homes))
    block = jnp.dot(
        blocks.astype(jnp.bfloat16),
        jnp.where(named, 1.0, 0.0).astype(jnp.bfloat16),
        preferred_element_type=jnp.float32,
    )[:1].astype(jnp.int32)
    place = lax.broadcasted_iota(jnp.int32, (slots, docs), 0)
    chosen = place == block * send_cap + rank
    chosen = jnp.where(chosen, 1.0, 0.0).astype(jnp.bfloat16)
    copies[-1].wait()
    rows = rows_ref[...]
    unit = rows * lax.rsqrt(jnp.sum(rows * rows, axis=1, keepdims=True) + EPS)
    high, rest = parts_of(unit)
    placed = jnp.dot(
        jnp.concatenate([chosen, chosen], axis=1),
        jnp.concatenate([high, rest.astype(jnp.bfloat16)], axis=0),
        preferred_element_type=jnp.float32,
    )
    for chunk in range(chunks):
        out_ref[pl.ds(chunk, slots, stride=chunks), :] = placed[
            :, chunk * LANES : (chunk + 1) * LANES
        ]
    for copy in copies[2:-1]:
        copy.wait()


def split_rows(rows_ref, high_ref, low_ref, send_cap):
    count, width = high_ref.shape
    chunks = width // LANES
    each = count // send_cap
    for rank in range(send_cap):
        for chunk in range(chunks):
            part = rows_ref[pl.ds(rank * chunks + chunk, each, stride=send_cap * chunks), :]
            high, rest = parts_of(part)
            cols = slice(chunk * LANES, (chunk + 1) * LANES)
            high_ref[rank * each : (rank + 1) * each, cols] = high
            low_ref[rank * each : (rank + 1) * each, cols] = rest.astype(jnp.bfloat16)


def across_lanes(column):
    wide = jnp.broadcast_to(column, (column.shape[0], LANES))
    return wide.T[:1, :]


def masked_max(scores, key_code, query_code, cap):
    first = query_code // cap * cap
    allowed = (key_code < query_code) & (key_code >= first)
    return jnp.max(jnp.where(allowed, scores, -1.0), axis=0, keepdims=True)


def best_of(key_high, key_low, high_turned, low_turned, key_code, query_code, cap):
    def dot(keys, queries):
        return jnp.dot(keys, queries, preferred_element_type=jnp.float32)

    scores = dot(key_high, high_turned) + (
        dot(key_high, low_turned) + dot(key_low, high_turned)
    )
    return masked_max(scores, key_code, query_code, cap)


def near_kernel(send_cap, table_ref, lists_ref, counts_ref, own_ref, high_ref, low_ref, best_ref,
                other_code_ref, query_code_ref, key_ref, own_high, own_low):
    cap = lists_ref.shape[1]
    key = jnp.broadcast_to(table_ref[:1], (LANES, table_ref.shape[1])).T[:, :1]
    key_ref[...] = key
    core = lax.axis_index("tiles").astype(jnp.int32)
    lists, counts = lists_ref[...], counts_ref[...]
    own_code = codes_of(lists, counts, core, key)
    query_code = across_lanes(own_code)
    query_code_ref[...] = query_code
    other_code_ref[...] = codes_of(lists, counts, 1 - core, key)
    split_rows(own_ref, own_high, own_low, send_cap)
    high, low = own_high[...], own_low[...]
    high_ref[...] = high.T
    low_ref[...] = low.T
    best_ref[...] = best_of(
        high, low, high_ref[...], low_ref[...], own_code, query_code, cap
    )


def far_kernel(send_cap, cap, high_ref, low_ref, best_ref, other_code_ref, query_code_ref,
               other_ref, out_ref):
    width, rows = high_ref.shape
    each = rows // send_cap
    chunks = width // LANES
    step = 2
    scores = jnp.zeros((rows, rows), jnp.float32)
    for begin in range(0, chunks, step):
        part = jnp.concatenate(
            [
                jnp.concatenate(
                    [
                        other_ref[pl.ds(rank * chunks + chunk, each, stride=send_cap * chunks), :]
                        for rank in range(send_cap)
                    ],
                    axis=0,
                )
                for chunk in range(begin, begin + step)
            ],
            axis=1,
        )
        high, rest = parts_of(part)
        low = rest.astype(jnp.bfloat16)
        span = slice(begin * LANES, (begin + step) * LANES)
        high_turned, low_turned = high_ref[span, :], low_ref[span, :]
        scores += (
            jnp.dot(high, high_turned, preferred_element_type=jnp.float32)
            + jnp.dot(high, low_turned, preferred_element_type=jnp.float32)
            + jnp.dot(low, high_turned, preferred_element_type=jnp.float32)
        )
    best = jnp.maximum(
        best_ref[...], masked_max(scores, other_code_ref[...], query_code_ref[...], cap)
    )
    lane = lax.broadcasted_iota(jnp.int32, (each, LANES), 1)
    out = jnp.zeros((each, LANES), jnp.float32)
    for rank in range(send_cap):
        column = jnp.broadcast_to(best[:, rank * each : (rank + 1) * each], (LANES, each)).T
        out = jnp.where(lane == rank, column, out)
    out_ref[...] = out


def pick_kernel(send_cap, slot_ref, key_ref, back_ref, out_ref):
    homes = back_ref.shape[0]
    docs = slot_ref.shape[1]
    slot, key, back = slot_ref[...], key_ref[...], back_ref[...]
    picked = jnp.zeros((homes, docs), jnp.float32)
    for rank in range(send_cap):
        value = jnp.broadcast_to(back[:, rank : rank + 1], (homes, docs))
        picked = jnp.where(slot == key[rank * homes : (rank + 1) * homes], value, picked)
    out_ref[...] = jnp.sum(picked, axis=0, keepdims=True)


def local(embeddings, cluster_of, row_lists, row_counts):
    n_docs = lax.axis_size("docs")
    n_tiles = lax.axis_size("tiles")
    doc_count, width = embeddings.shape
    send_cap = n_tiles * doc_count // n_docs
    cl_local = row_lists.shape[0]
    slots = n_docs * send_cap
    flat = (slots * width // LANES, LANES)
    vmem = pl.BlockSpec(memory_space=pltpu.VMEM)

    hbm = pl.BlockSpec(memory_space=pltpu.HBM)

    def in_hbm(array):
        return pltpu.with_memory_space_constraint(array, pltpu.HBM)

    order = group_order()
    table = np.zeros((2, slots), np.int32)
    table[0] = [home * send_cap + rank for rank in range(send_cap) for home in order]
    table[1, order] = range(n_docs)
    outgoing, slot, blocks, lists, counts = pl.pallas_call(
        functools.partial(prep_kernel, cl_local, send_cap),
        out_shape=(
            jax.ShapeDtypeStruct(flat, jnp.float32),
            jax.ShapeDtypeStruct((1, doc_count), jnp.int32),
            jax.ShapeDtypeStruct(table.shape, jnp.int32),
            jax.ShapeDtypeStruct(row_lists.shape, jnp.int32),
            jax.ShapeDtypeStruct((1, cl_local), jnp.int32),
        ),
        in_specs=[hbm] * 5,
        out_specs=(vmem,) * 5,
        scratch_shapes=[
            pltpu.VMEM((1, doc_count), jnp.int32),
            pltpu.VMEM((doc_count, width), jnp.float32),
            pltpu.SemaphoreType.DMA((5,)),
        ],
        compiler_params=PARAMS,
        name="prep",
    )(
        in_hbm(jnp.asarray(table)),
        in_hbm(cluster_of.reshape(1, doc_count)),
        in_hbm(row_lists),
        in_hbm(row_counts.reshape(1, cl_local)),
        in_hbm(embeddings),
    )

    def exchange(blocks):
        return lax.all_to_all(
            blocks, "docs", split_axis=0, concat_axis=0, tiled=True,
            axis_index_groups=[order],
        )

    own = exchange(outgoing.reshape(n_docs, -1, LANES)).reshape(flat)
    other = lax.ppermute(own, "tiles", [(0, 1), (1, 0)])

    cap = row_lists.shape[1]
    turned = jax.ShapeDtypeStruct((width, slots), jnp.bfloat16)
    parts = [pltpu.VMEM((slots, width), jnp.bfloat16)] * 2
    *near, key = pl.pallas_call(
        functools.partial(near_kernel, send_cap),
        out_shape=(
            turned,
            turned,
            jax.ShapeDtypeStruct((1, slots), jnp.float32),
            jax.ShapeDtypeStruct((slots, 1), jnp.int32),
            jax.ShapeDtypeStruct((1, slots), jnp.int32),
            jax.ShapeDtypeStruct((slots, 1), jnp.int32),
        ),
        in_specs=[vmem] * 4,
        out_specs=(vmem,) * 6,
        scratch_shapes=parts,
        compiler_params=PARAMS,
        name="near",
    )(blocks, lists, counts, own)
    best = pl.pallas_call(
        functools.partial(far_kernel, send_cap, cap),
        out_shape=jax.ShapeDtypeStruct((n_docs, LANES), jnp.float32),
        in_specs=[vmem] * 6,
        out_specs=vmem,
        compiler_params=PARAMS,
        name="far",
    )(*near, other)

    back = exchange(best.reshape(n_docs, 1, LANES)).reshape(n_docs, LANES)
    picked = pl.pallas_call(
        functools.partial(pick_kernel, send_cap),
        out_shape=jax.ShapeDtypeStruct((1, doc_count), jnp.float32),
        in_specs=[vmem] * 3,
        out_specs=vmem,
        compiler_params=PARAMS,
        name="pick",
    )(slot, key, back)
    return picked.reshape(doc_count)


def solution(mesh):
    placed = (P(("docs", "tiles"), None), P(("docs", "tiles")), P("docs", None), P("docs"))
    return jax.shard_map(
        local, mesh=mesh, in_specs=placed, out_specs=P(("docs", "tiles")), check_vma=False
    )
```

```python
import functools

import jax
import jax.numpy as jnp
import numpy as np
from jax import lax
from jax.experimental import pallas as pl
from jax.experimental.pallas import tpu as pltpu
from jax.sharding import PartitionSpec as P

EPS = 1e-06
LANES = 128
GRID = (8, 4, 4)
PARAMS = pltpu.CompilerParams(vmem_limit_bytes=32 * 1024 * 1024)


def group_order(ahead):
    spots = [
        (z, x, y) for z in range(GRID[0]) for x in range(GRID[1]) for y in range(GRID[2])
    ]
    first = (GRID[0] // 2 + ahead, GRID[1] // 2, GRID[2] // 2)

    def distance(spot):
        gaps = [abs(at - start) for at, start in zip(spot, first)]
        return sum(min(gap, size - gap) for gap, size in zip(gaps, GRID))

    return sorted(
        range(len(spots)), key=lambda index: (distance(spots[index]) > 0, -distance(spots[index]))
    )


def parts_of(rows):
    high = rows.astype(jnp.bfloat16)
    rest = rows - high.astype(jnp.float32)
    return high, rest


def codes_of(lists, counts, half, key):
    cap = lists.shape[1]
    rows = key.shape[0]
    place = half * rows + key
    position = lax.broadcasted_iota(jnp.int32, (1, cap), 1)
    code = jnp.full((rows, cap), -1, jnp.int32)
    for cluster in range(lists.shape[0]):
        listed = jnp.where(position < counts[:, cluster : cluster + 1],
                           lists[cluster : cluster + 1, :], -1)
        code = jnp.where(listed == place, position + cluster * cap, code)
    return jnp.max(code, axis=1, keepdims=True)


def prep_kernel(cl_local, send_cap, table_hbm, cluster_hbm, lists_hbm, counts_hbm, rows_hbm,
                out_ref, slot_ref, table_ref, lists_ref, counts_ref,
                cluster_ref, rows_ref, sems):
    docs, width = rows_ref.shape
    slots = out_ref.shape[0] * LANES // width
    chunks = width // LANES
    copies = [
        pltpu.make_async_copy(source, target, sems.at[index])
        for index, (source, target) in enumerate(
            (
                (cluster_hbm, cluster_ref),
                (table_hbm, table_ref),
                (lists_hbm, lists_ref),
                (counts_hbm, counts_ref),
                (rows_hbm, rows_ref),
            )
        )
    ]
    for copy in copies:
        copy.start()
    for copy in copies[:2]:
        copy.wait()
    home = lax.shift_right_logical(cluster_ref[...], cl_local.bit_length() - 1)
    across = jnp.broadcast_to(home, (docs, docs))
    down = across.T
    sub = lax.broadcasted_iota(jnp.int32, (docs, docs), 0)
    lane = lax.broadcasted_iota(jnp.int32, (docs, docs), 1)
    before = jnp.where((across == down) & (sub < lane), 1, 0)
    rank = jnp.sum(before, axis=0, keepdims=True)
    slot_ref[...] = home * send_cap + rank
    homes = slots // send_cap
    core = lax.axis_index("tiles").astype(jnp.int32)
    blocks = jnp.where(core == 0, table_ref[3:4, :homes], table_ref[4:5, :homes])
    named = lax.broadcasted_iota(jnp.int32, (homes, docs), 0) == home
    blocks = jnp.broadcast_to(blocks.astype(jnp.float32), (8, homes))
    block = jnp.dot(
        blocks.astype(jnp.bfloat16),
        jnp.where(named, 1.0, 0.0).astype(jnp.bfloat16),
        preferred_element_type=jnp.float32,
    )[:1].astype(jnp.int32)
    place = lax.broadcasted_iota(jnp.int32, (slots, docs), 0)
    chosen = place == block * send_cap + rank
    chosen = jnp.where(chosen, 1.0, 0.0).astype(jnp.bfloat16)
    copies[-1].wait()
    rows = rows_ref[...]
    unit = rows * lax.rsqrt(jnp.sum(rows * rows, axis=1, keepdims=True) + EPS)
    high, rest = parts_of(unit)
    placed = jnp.dot(
        jnp.concatenate([chosen, chosen], axis=1),
        jnp.concatenate([high, rest.astype(jnp.bfloat16)], axis=0),
        preferred_element_type=jnp.float32,
    )
    for chunk in range(chunks):
        out_ref[pl.ds(chunk, slots, stride=chunks), :] = placed[
            :, chunk * LANES : (chunk + 1) * LANES
        ]
    for copy in copies[2:-1]:
        copy.wait()


def split_rows(rows_ref, high_ref, low_ref, send_cap):
    count, width = high_ref.shape
    chunks = width // LANES
    each = count // send_cap
    for rank in range(send_cap):
        for chunk in range(chunks):
            part = rows_ref[pl.ds(rank * chunks + chunk, each, stride=send_cap * chunks), :]
            high, rest = parts_of(part)
            cols = slice(chunk * LANES, (chunk + 1) * LANES)
            high_ref[rank * each : (rank + 1) * each, cols] = high
            low_ref[rank * each : (rank + 1) * each, cols] = rest.astype(jnp.bfloat16)


def across_lanes(column):
    wide = jnp.broadcast_to(column, (column.shape[0], LANES))
    return wide.T[:1, :]


def masked_max(scores, key_code, query_code, cap):
    first = query_code // cap * cap
    allowed = (key_code < query_code) & (key_code >= first)
    return jnp.max(jnp.where(allowed, scores, -1.0), axis=0, keepdims=True)


def best_of(key_high, key_low, high_turned, low_turned, key_code, query_code, cap):
    def dot(keys, queries):
        return jnp.dot(keys, queries, preferred_element_type=jnp.float32)

    scores = dot(key_high, high_turned) + (
        dot(key_high, low_turned) + dot(key_low, high_turned)
    )
    return masked_max(scores, key_code, query_code, cap)


def down_rows(row):
    return jnp.broadcast_to(row, (LANES, row.shape[1])).T[:, :1]


def turned(rows, turn):
    return lax.dot_general(
        rows, turn, (((0,), (0,)), ((), ())), preferred_element_type=jnp.float32
    ).astype(jnp.bfloat16)


def near_kernel(send_cap, table_ref, lists_ref, counts_ref, own_ref, high_ref, low_ref, best_ref,
                other_code_ref, query_code_ref, key_ref, own_high, own_low):
    cap = lists_ref.shape[1]
    core = lax.axis_index("tiles").astype(jnp.int32)
    back, one, two = (table_ref[row : row + 1] for row in range(3))
    own = down_rows(jnp.where(core == 0, one, two))
    other = down_rows(jnp.where(core == 0, two, one))
    key = down_rows(back)
    key_ref[...] = key
    lists, counts = lists_ref[...], counts_ref[...]
    own_code = codes_of(lists, counts, core, own)
    query_code = across_lanes(codes_of(lists, counts, core, key))
    query_code_ref[...] = query_code
    other_code_ref[...] = codes_of(lists, counts, 1 - core, other)
    turn = jnp.where(own == back, 1.0, 0.0).astype(jnp.bfloat16)
    split_rows(own_ref, own_high, own_low, send_cap)
    high, low = own_high[...], own_low[...]
    high_ref[...] = turned(high, turn)
    low_ref[...] = turned(low, turn)
    best_ref[...] = best_of(
        high, low, high_ref[...], low_ref[...], own_code, query_code, cap
    )


def far_kernel(send_cap, cap, high_ref, low_ref, best_ref, other_code_ref, query_code_ref,
               other_ref, out_ref):
    width, rows = high_ref.shape
    each = rows // send_cap
    chunks = width // LANES
    step = 2
    scores = jnp.zeros((rows, rows), jnp.float32)
    for begin in range(0, chunks, step):
        part = jnp.concatenate(
            [
                jnp.concatenate(
                    [
                        other_ref[pl.ds(rank * chunks + chunk, each, stride=send_cap * chunks), :]
                        for rank in range(send_cap)
                    ],
                    axis=0,
                )
                for chunk in range(begin, begin + step)
            ],
            axis=1,
        )
        high, rest = parts_of(part)
        low = rest.astype(jnp.bfloat16)
        span = slice(begin * LANES, (begin + step) * LANES)
        high_turned, low_turned = high_ref[span, :], low_ref[span, :]
        scores += (
            jnp.dot(high, high_turned, preferred_element_type=jnp.float32)
            + jnp.dot(high, low_turned, preferred_element_type=jnp.float32)
            + jnp.dot(low, high_turned, preferred_element_type=jnp.float32)
        )
    best = jnp.maximum(
        best_ref[...], masked_max(scores, other_code_ref[...], query_code_ref[...], cap)
    )
    lane = lax.broadcasted_iota(jnp.int32, (each, LANES), 1)
    out = jnp.zeros((each, LANES), jnp.float32)
    for rank in range(send_cap):
        column = jnp.broadcast_to(best[:, rank * each : (rank + 1) * each], (LANES, each)).T
        out = jnp.where(lane == rank, column, out)
    out_ref[...] = out


def pick_kernel(send_cap, slot_ref, key_ref, back_ref, out_ref):
    homes = back_ref.shape[0]
    docs = slot_ref.shape[1]
    slot, key, back = slot_ref[...], key_ref[...], back_ref[...]
    picked = jnp.zeros((homes, docs), jnp.float32)
    for rank in range(send_cap):
        value = jnp.broadcast_to(back[:, rank : rank + 1], (homes, docs))
        picked = jnp.where(slot == key[rank * homes : (rank + 1) * homes], value, picked)
    out_ref[...] = jnp.sum(picked, axis=0, keepdims=True)


def local(embeddings, cluster_of, row_lists, row_counts):
    n_docs = lax.axis_size("docs")
    n_tiles = lax.axis_size("tiles")
    doc_count, width = embeddings.shape
    send_cap = n_tiles * doc_count // n_docs
    cl_local = row_lists.shape[0]
    slots = n_docs * send_cap
    flat = (slots * width // LANES, LANES)
    vmem = pl.BlockSpec(memory_space=pltpu.VMEM)

    hbm = pl.BlockSpec(memory_space=pltpu.HBM)

    def in_hbm(array):
        return pltpu.with_memory_space_constraint(array, pltpu.HBM)

    order = group_order(0)
    firsts = [group_order(core) for core in range(n_tiles)]
    table = np.zeros((1 + 2 * n_tiles, slots), np.int32)
    for row, homes in enumerate([order] + firsts):
        table[row] = [home * send_cap + rank for rank in range(send_cap) for home in homes]
    for core, homes in enumerate(firsts):
        table[1 + n_tiles + core, homes] = range(n_docs)
    outgoing, slot, blocks, lists, counts = pl.pallas_call(
        functools.partial(prep_kernel, cl_local, send_cap),
        out_shape=(
            jax.ShapeDtypeStruct(flat, jnp.float32),
            jax.ShapeDtypeStruct((1, doc_count), jnp.int32),
            jax.ShapeDtypeStruct(table.shape, jnp.int32),
            jax.ShapeDtypeStruct(row_lists.shape, jnp.int32),
            jax.ShapeDtypeStruct((1, cl_local), jnp.int32),
        ),
        in_specs=[hbm] * 5,
        out_specs=(vmem,) * 5,
        scratch_shapes=[
            pltpu.VMEM((1, doc_count), jnp.int32),
            pltpu.VMEM((doc_count, width), jnp.float32),
            pltpu.SemaphoreType.DMA((5,)),
        ],
        compiler_params=PARAMS,
        name="prep",
    )(
        in_hbm(jnp.asarray(table)),
        in_hbm(cluster_of.reshape(1, doc_count)),
        in_hbm(row_lists),
        in_hbm(row_counts.reshape(1, cl_local)),
        in_hbm(embeddings),
    )

    def exchange(blocks, axis, groups):
        return lax.all_to_all(
            blocks, axis, split_axis=0, concat_axis=0, tiled=True, axis_index_groups=groups
        )

    groups = [[home * n_tiles + core for home in homes] for core, homes in enumerate(firsts)]
    own = exchange(outgoing.reshape(n_docs, -1, LANES), ("docs", "tiles"), groups)
    own = own.reshape(flat)
    other = lax.ppermute(own, "tiles", [(0, 1), (1, 0)])

    cap = row_lists.shape[1]
    turned = jax.ShapeDtypeStruct((width, slots), jnp.bfloat16)
    parts = [pltpu.VMEM((slots, width), jnp.bfloat16)] * 2
    *near, key = pl.pallas_call(
        functools.partial(near_kernel, send_cap),
        out_shape=(
            turned,
            turned,
            jax.ShapeDtypeStruct((1, slots), jnp.float32),
            jax.ShapeDtypeStruct((slots, 1), jnp.int32),
            jax.ShapeDtypeStruct((1, slots), jnp.int32),
            jax.ShapeDtypeStruct((slots, 1), jnp.int32),
        ),
        in_specs=[vmem] * 4,
        out_specs=(vmem,) * 6,
        scratch_shapes=parts,
        compiler_params=PARAMS,
        name="near",
    )(blocks, lists, counts, own)
    best = pl.pallas_call(
        functools.partial(far_kernel, send_cap, cap),
        out_shape=jax.ShapeDtypeStruct((n_docs, LANES), jnp.float32),
        in_specs=[vmem] * 6,
        out_specs=vmem,
        compiler_params=PARAMS,
        name="far",
    )(*near, other)

    back = exchange(best.reshape(n_docs, 1, LANES), "docs", [order]).reshape(n_docs, LANES)
    picked = pl.pallas_call(
        functools.partial(pick_kernel, send_cap),
        out_shape=jax.ShapeDtypeStruct((1, doc_count), jnp.float32),
        in_specs=[vmem] * 3,
        out_specs=vmem,
        compiler_params=PARAMS,
        name="pick",
    )(slot, key, back)
    return picked.reshape(doc_count)


def solution(mesh):
    placed = (P(("docs", "tiles"), None), P(("docs", "tiles")), P("docs", None), P("docs"))
    return jax.shard_map(
        local, mesh=mesh, in_specs=placed, out_specs=P(("docs", "tiles")), check_vma=False
    )
```

```python
import functools

import jax
import jax.numpy as jnp
import numpy as np
from jax import lax
from jax.experimental import pallas as pl
from jax.experimental.pallas import tpu as pltpu
from jax.sharding import PartitionSpec as P

EPS = 1e-06
LANES = 128
GRID = (8, 4, 4)
PARAMS = pltpu.CompilerParams(vmem_limit_bytes=32 * 1024 * 1024)


def group_order(ahead):
    spots = [
        (z, x, y) for z in range(GRID[0]) for x in range(GRID[1]) for y in range(GRID[2])
    ]
    first = (GRID[0] // 2 + ahead, GRID[1] // 2, GRID[2] // 2)

    def distance(spot):
        gaps = [abs(at - start) for at, start in zip(spot, first)]
        return sum(min(gap, size - gap) for gap, size in zip(gaps, GRID))

    return sorted(
        range(len(spots)), key=lambda index: (distance(spots[index]) > 0, -distance(spots[index]))
    )


def return_order():
    count = GRID[0] * GRID[1] * GRID[2]
    bits = count.bit_length() - 1
    first = group_order(0)[0]
    return [
        first ^ sum((index >> bit & 1) << (bits - 1 - bit) for bit in range(bits))
        for index in range(count)
    ]


def parts_of(rows):
    high = rows.astype(jnp.bfloat16)
    rest = rows - high.astype(jnp.float32)
    return high, rest


def codes_of(lists, counts, half, key):
    cap = lists.shape[1]
    rows = key.shape[0]
    place = half * rows + key
    position = lax.broadcasted_iota(jnp.int32, (1, cap), 1)
    code = jnp.full((rows, cap), -1, jnp.int32)
    for cluster in range(lists.shape[0]):
        listed = jnp.where(position < counts[:, cluster : cluster + 1],
                           lists[cluster : cluster + 1, :], -1)
        code = jnp.where(listed == place, position + cluster * cap, code)
    return jnp.max(code, axis=1, keepdims=True)


def prep_kernel(cl_local, send_cap, table_hbm, cluster_hbm, lists_hbm, counts_hbm, rows_hbm,
                out_ref, slot_ref, table_ref, lists_ref, counts_ref,
                cluster_ref, rows_ref, sems):
    docs, width = rows_ref.shape
    slots = out_ref.shape[0] * LANES // width
    chunks = width // LANES
    copies = [
        pltpu.make_async_copy(source, target, sems.at[index])
        for index, (source, target) in enumerate(
            (
                (cluster_hbm, cluster_ref),
                (table_hbm, table_ref),
                (lists_hbm, lists_ref),
                (counts_hbm, counts_ref),
                (rows_hbm, rows_ref),
            )
        )
    ]
    for copy in copies:
        copy.start()
    for copy in copies[:2]:
        copy.wait()
    home = lax.shift_right_logical(cluster_ref[...], cl_local.bit_length() - 1)
    across = jnp.broadcast_to(home, (docs, docs))
    down = across.T
    sub = lax.broadcasted_iota(jnp.int32, (docs, docs), 0)
    lane = lax.broadcasted_iota(jnp.int32, (docs, docs), 1)
    before = jnp.where((across == down) & (sub < lane), 1, 0)
    rank = jnp.sum(before, axis=0, keepdims=True)
    slot_ref[...] = home * send_cap + rank
    homes = slots // send_cap
    core = lax.axis_index("tiles").astype(jnp.int32)
    blocks = jnp.where(core == 0, table_ref[3:4, :homes], table_ref[4:5, :homes])
    named = lax.broadcasted_iota(jnp.int32, (homes, docs), 0) == home
    blocks = jnp.broadcast_to(blocks.astype(jnp.float32), (8, homes))
    block = jnp.dot(
        blocks.astype(jnp.bfloat16),
        jnp.where(named, 1.0, 0.0).astype(jnp.bfloat16),
        preferred_element_type=jnp.float32,
    )[:1].astype(jnp.int32)
    place = lax.broadcasted_iota(jnp.int32, (slots, docs), 0)
    chosen = place == block * send_cap + rank
    chosen = jnp.where(chosen, 1.0, 0.0).astype(jnp.bfloat16)
    copies[-1].wait()
    rows = rows_ref[...]
    unit = rows * lax.rsqrt(jnp.sum(rows * rows, axis=1, keepdims=True) + EPS)
    high, rest = parts_of(unit)
    placed = jnp.dot(
        jnp.concatenate([chosen, chosen], axis=1),
        jnp.concatenate([high, rest.astype(jnp.bfloat16)], axis=0),
        preferred_element_type=jnp.float32,
    )
    for chunk in range(chunks):
        out_ref[pl.ds(chunk, slots, stride=chunks), :] = placed[
            :, chunk * LANES : (chunk + 1) * LANES
        ]
    for copy in copies[2:-1]:
        copy.wait()


def split_rows(rows_ref, high_ref, low_ref, send_cap):
    count, width = high_ref.shape
    chunks = width // LANES
    each = count // send_cap
    for rank in range(send_cap):
        for chunk in range(chunks):
            part = rows_ref[pl.ds(rank * chunks + chunk, each, stride=send_cap * chunks), :]
            high, rest = parts_of(part)
            cols = slice(chunk * LANES, (chunk + 1) * LANES)
            high_ref[rank * each : (rank + 1) * each, cols] = high
            low_ref[rank * each : (rank + 1) * each, cols] = rest.astype(jnp.bfloat16)


def across_lanes(column):
    wide = jnp.broadcast_to(column, (column.shape[0], LANES))
    return wide.T[:1, :]


def masked_max(scores, key_code, query_code, cap):
    first = query_code // cap * cap
    allowed = (key_code < query_code) & (key_code >= first)
    return jnp.max(jnp.where(allowed, scores, -1.0), axis=0, keepdims=True)


def best_of(key_high, key_low, high_turned, low_turned, key_code, query_code, cap):
    def dot(keys, queries):
        return jnp.dot(keys, queries, preferred_element_type=jnp.float32)

    scores = dot(key_high, high_turned) + (
        dot(key_high, low_turned) + dot(key_low, high_turned)
    )
    return masked_max(scores, key_code, query_code, cap)


def down_rows(row):
    return jnp.broadcast_to(row, (LANES, row.shape[1])).T[:, :1]


def turned(rows, turn):
    return lax.dot_general(
        rows, turn, (((0,), (0,)), ((), ())), preferred_element_type=jnp.float32
    ).astype(jnp.bfloat16)


def near_kernel(send_cap, table_ref, lists_ref, counts_ref, own_ref, high_ref, low_ref, best_ref,
                other_code_ref, query_code_ref, key_ref, own_high, own_low):
    cap = lists_ref.shape[1]
    core = lax.axis_index("tiles").astype(jnp.int32)
    back, one, two = (table_ref[row : row + 1] for row in range(3))
    own = down_rows(jnp.where(core == 0, one, two))
    other = down_rows(jnp.where(core == 0, two, one))
    key = down_rows(back)
    key_ref[...] = key
    lists, counts = lists_ref[...], counts_ref[...]
    own_code = codes_of(lists, counts, core, own)
    query_code = across_lanes(codes_of(lists, counts, core, key))
    query_code_ref[...] = query_code
    other_code_ref[...] = codes_of(lists, counts, 1 - core, other)
    turn = jnp.where(own == back, 1.0, 0.0).astype(jnp.bfloat16)
    split_rows(own_ref, own_high, own_low, send_cap)
    high, low = own_high[...], own_low[...]
    high_ref[...] = turned(high, turn)
    low_ref[...] = turned(low, turn)
    best_ref[...] = best_of(
        high, low, high_ref[...], low_ref[...], own_code, query_code, cap
    )


def far_kernel(send_cap, cap, high_ref, low_ref, best_ref, other_code_ref, query_code_ref,
               other_ref, out_ref):
    width, rows = high_ref.shape
    each = rows // send_cap
    chunks = width // LANES
    step = 2
    scores = jnp.zeros((rows, rows), jnp.float32)
    for begin in range(0, chunks, step):
        part = jnp.concatenate(
            [
                jnp.concatenate(
                    [
                        other_ref[pl.ds(rank * chunks + chunk, each, stride=send_cap * chunks), :]
                        for rank in range(send_cap)
                    ],
                    axis=0,
                )
                for chunk in range(begin, begin + step)
            ],
            axis=1,
        )
        high, rest = parts_of(part)
        low = rest.astype(jnp.bfloat16)
        span = slice(begin * LANES, (begin + step) * LANES)
        high_turned, low_turned = high_ref[span, :], low_ref[span, :]
        scores += (
            jnp.dot(high, high_turned, preferred_element_type=jnp.float32)
            + jnp.dot(high, low_turned, preferred_element_type=jnp.float32)
            + jnp.dot(low, high_turned, preferred_element_type=jnp.float32)
        )
    best = jnp.maximum(
        best_ref[...], masked_max(scores, other_code_ref[...], query_code_ref[...], cap)
    )
    lane = lax.broadcasted_iota(jnp.int32, (each, LANES), 1)
    out = jnp.zeros((each, LANES), jnp.float32)
    for rank in range(send_cap):
        column = jnp.broadcast_to(best[:, rank * each : (rank + 1) * each], (LANES, each)).T
        out = jnp.where(lane == rank, column, out)
    out_ref[...] = out


def pick_kernel(send_cap, slot_ref, key_ref, back_ref, out_ref):
    homes = back_ref.shape[0]
    docs = slot_ref.shape[1]
    slot, key, back = slot_ref[...], key_ref[...], back_ref[...]
    picked = jnp.zeros((homes, docs), jnp.float32)
    for rank in range(send_cap):
        value = jnp.broadcast_to(back[:, rank : rank + 1], (homes, docs))
        picked = jnp.where(slot == key[rank * homes : (rank + 1) * homes], value, picked)
    out_ref[...] = jnp.sum(picked, axis=0, keepdims=True)


def local(embeddings, cluster_of, row_lists, row_counts):
    n_docs = lax.axis_size("docs")
    n_tiles = lax.axis_size("tiles")
    doc_count, width = embeddings.shape
    send_cap = n_tiles * doc_count // n_docs
    cl_local = row_lists.shape[0]
    slots = n_docs * send_cap
    flat = (slots * width // LANES, LANES)
    vmem = pl.BlockSpec(memory_space=pltpu.VMEM)

    hbm = pl.BlockSpec(memory_space=pltpu.HBM)

    def in_hbm(array):
        return pltpu.with_memory_space_constraint(array, pltpu.HBM)

    order = return_order()
    firsts = [group_order(core) for core in range(n_tiles)]
    table = np.zeros((1 + 2 * n_tiles, slots), np.int32)
    for row, homes in enumerate([order] + firsts):
        table[row] = [home * send_cap + rank for rank in range(send_cap) for home in homes]
    for core, homes in enumerate(firsts):
        table[1 + n_tiles + core, homes] = range(n_docs)
    outgoing, slot, blocks, lists, counts = pl.pallas_call(
        functools.partial(prep_kernel, cl_local, send_cap),
        out_shape=(
            jax.ShapeDtypeStruct(flat, jnp.float32),
            jax.ShapeDtypeStruct((1, doc_count), jnp.int32),
            jax.ShapeDtypeStruct(table.shape, jnp.int32),
            jax.ShapeDtypeStruct(row_lists.shape, jnp.int32),
            jax.ShapeDtypeStruct((1, cl_local), jnp.int32),
        ),
        in_specs=[hbm] * 5,
        out_specs=(vmem,) * 5,
        scratch_shapes=[
            pltpu.VMEM((1, doc_count), jnp.int32),
            pltpu.VMEM((doc_count, width), jnp.float32),
            pltpu.SemaphoreType.DMA((5,)),
        ],
        compiler_params=PARAMS,
        name="prep",
    )(
        in_hbm(jnp.asarray(table)),
        in_hbm(cluster_of.reshape(1, doc_count)),
        in_hbm(row_lists),
        in_hbm(row_counts.reshape(1, cl_local)),
        in_hbm(embeddings),
    )

    def exchange(blocks, axis, groups):
        return lax.all_to_all(
            blocks, axis, split_axis=0, concat_axis=0, tiled=True, axis_index_groups=groups
        )

    groups = [[home * n_tiles + core for home in homes] for core, homes in enumerate(firsts)]
    own = exchange(outgoing.reshape(n_docs, -1, LANES), ("docs", "tiles"), groups)
    own = own.reshape(flat)
    other = lax.ppermute(own, "tiles", [(0, 1), (1, 0)])

    cap = row_lists.shape[1]
    turned = jax.ShapeDtypeStruct((width, slots), jnp.bfloat16)
    parts = [pltpu.VMEM((slots, width), jnp.bfloat16)] * 2
    *near, key = pl.pallas_call(
        functools.partial(near_kernel, send_cap),
        out_shape=(
            turned,
            turned,
            jax.ShapeDtypeStruct((1, slots), jnp.float32),
            jax.ShapeDtypeStruct((slots, 1), jnp.int32),
            jax.ShapeDtypeStruct((1, slots), jnp.int32),
            jax.ShapeDtypeStruct((slots, 1), jnp.int32),
        ),
        in_specs=[vmem] * 4,
        out_specs=(vmem,) * 6,
        scratch_shapes=parts,
        compiler_params=PARAMS,
        name="near",
    )(blocks, lists, counts, own)
    best = pl.pallas_call(
        functools.partial(far_kernel, send_cap, cap),
        out_shape=jax.ShapeDtypeStruct((n_docs, LANES), jnp.float32),
        in_specs=[vmem] * 6,
        out_specs=vmem,
        compiler_params=PARAMS,
        name="far",
    )(*near, other)

    back = exchange(best.reshape(n_docs, 1, LANES), "docs", [order]).reshape(n_docs, LANES)
    picked = pl.pallas_call(
        functools.partial(pick_kernel, send_cap),
        out_shape=jax.ShapeDtypeStruct((1, doc_count), jnp.float32),
        in_specs=[vmem] * 3,
        out_specs=vmem,
        compiler_params=PARAMS,
        name="pick",
    )(slot, key, back)
    return picked.reshape(doc_count)


def solution(mesh):
    placed = (P(("docs", "tiles"), None), P(("docs", "tiles")), P("docs", None), P("docs"))
    return jax.shard_map(
        local, mesh=mesh, in_specs=placed, out_specs=P(("docs", "tiles")), check_vma=False
    )
```

```python
import functools

import jax
import jax.numpy as jnp
import numpy as np
from jax import lax
from jax.experimental import pallas as pl
from jax.experimental.pallas import tpu as pltpu
from jax.sharding import PartitionSpec as P

EPS = 1e-06
LANES = 128
GRID = (8, 4, 4)
PARAMS = pltpu.CompilerParams(vmem_limit_bytes=32 * 1024 * 1024)


def group_order(ahead):
    spots = [
        (z, x, y) for z in range(GRID[0]) for x in range(GRID[1]) for y in range(GRID[2])
    ]
    first = (GRID[0] // 2 + ahead, GRID[1] // 2, GRID[2] // 2)

    def distance(spot):
        gaps = [abs(at - start) for at, start in zip(spot, first)]
        return sum(min(gap, size - gap) for gap, size in zip(gaps, GRID))

    return sorted(
        range(len(spots)), key=lambda index: (distance(spots[index]) > 0, -distance(spots[index]))
    )


def return_order():
    count = GRID[0] * GRID[1] * GRID[2]
    bits = count.bit_length() - 1
    first = group_order(0)[0]
    return [
        first ^ sum((index >> bit & 1) << (bits - 1 - bit) for bit in range(bits))
        for index in range(count)
    ]


def parts_of(rows):
    high = rows.astype(jnp.bfloat16)
    rest = rows - high.astype(jnp.float32)
    return high, rest


def codes_of(lists, counts, half, key):
    cap = lists.shape[1]
    rows = key.shape[0]
    place = half * rows + key
    position = lax.broadcasted_iota(jnp.int32, (1, cap), 1)
    code = jnp.full((rows, cap), -1, jnp.int32)
    for cluster in range(lists.shape[0]):
        listed = jnp.where(position < counts[:, cluster : cluster + 1],
                           lists[cluster : cluster + 1, :], -1)
        code = jnp.where(listed == place, position + cluster * cap, code)
    return jnp.max(code, axis=1, keepdims=True)


def prep_kernel(cl_local, send_cap, table_hbm, cluster_hbm, lists_hbm, counts_hbm, rows_hbm,
                out_ref, slot_ref, table_ref, lists_ref, counts_ref,
                cluster_ref, rows_ref, sems):
    docs, width = rows_ref.shape
    slots = out_ref.shape[0] * LANES // width
    chunks = width // LANES
    copies = [
        pltpu.make_async_copy(source, target, sems.at[index])
        for index, (source, target) in enumerate(
            (
                (cluster_hbm, cluster_ref),
                (table_hbm, table_ref),
                (lists_hbm, lists_ref),
                (counts_hbm, counts_ref),
                (rows_hbm, rows_ref),
            )
        )
    ]
    for copy in copies:
        copy.start()
    for copy in copies[:2]:
        copy.wait()
    home = lax.shift_right_logical(cluster_ref[...], cl_local.bit_length() - 1)
    across = jnp.broadcast_to(home, (docs, docs))
    down = across.T
    sub = lax.broadcasted_iota(jnp.int32, (docs, docs), 0)
    lane = lax.broadcasted_iota(jnp.int32, (docs, docs), 1)
    before = jnp.where((across == down) & (sub < lane), 1, 0)
    rank = jnp.sum(before, axis=0, keepdims=True)
    slot_ref[...] = home * send_cap + rank
    homes = slots // send_cap
    core = lax.axis_index("tiles").astype(jnp.int32)
    blocks = jnp.where(core == 0, table_ref[3:4, :homes], table_ref[4:5, :homes])
    named = lax.broadcasted_iota(jnp.int32, (homes, docs), 0) == home
    blocks = jnp.broadcast_to(blocks.astype(jnp.float32), (8, homes))
    block = jnp.dot(
        blocks.astype(jnp.bfloat16),
        jnp.where(named, 1.0, 0.0).astype(jnp.bfloat16),
        preferred_element_type=jnp.float32,
    )[:1].astype(jnp.int32)
    place = lax.broadcasted_iota(jnp.int32, (slots, docs), 0)
    chosen = place == block * send_cap + rank
    chosen = jnp.where(chosen, 1.0, 0.0).astype(jnp.bfloat16)
    copies[-1].wait()
    rows = rows_ref[...]
    unit = rows * lax.rsqrt(jnp.sum(rows * rows, axis=1, keepdims=True) + EPS)
    high, rest = parts_of(unit)
    placed = jnp.dot(
        jnp.concatenate([chosen, chosen], axis=1),
        jnp.concatenate([high, rest.astype(jnp.bfloat16)], axis=0),
        preferred_element_type=jnp.float32,
    )
    for chunk in range(chunks):
        out_ref[pl.ds(chunk, slots, stride=chunks), :] = placed[
            :, chunk * LANES : (chunk + 1) * LANES
        ]
    for copy in copies[2:-1]:
        copy.wait()


def split_rows(rows_ref, high_ref, low_ref, send_cap):
    count, width = high_ref.shape
    chunks = width // LANES
    each = count // send_cap
    for rank in range(send_cap):
        for chunk in range(chunks):
            part = rows_ref[pl.ds(rank * chunks + chunk, each, stride=send_cap * chunks), :]
            high, rest = parts_of(part)
            cols = slice(chunk * LANES, (chunk + 1) * LANES)
            high_ref[rank * each : (rank + 1) * each, cols] = high
            low_ref[rank * each : (rank + 1) * each, cols] = rest.astype(jnp.bfloat16)


def across_lanes(column):
    wide = jnp.broadcast_to(column, (column.shape[0], LANES))
    return wide.T[:1, :]


def masked_max(scores, key_code, query_code, cap):
    first = query_code // cap * cap
    allowed = (key_code < query_code) & (key_code >= first)
    return jnp.max(jnp.where(allowed, scores, -1.0), axis=0, keepdims=True)


def best_of(key_high, key_low, high_turned, low_turned, key_code, query_code, cap):
    def dot(keys, queries):
        return jnp.dot(keys, queries, preferred_element_type=jnp.float32)

    scores = dot(key_high, high_turned) + (
        dot(key_high, low_turned) + dot(key_low, high_turned)
    )
    return masked_max(scores, key_code, query_code, cap)


def down_rows(row):
    return jnp.broadcast_to(row, (LANES, row.shape[1])).T


def turned(rows, turn):
    return lax.dot_general(
        rows, turn, (((0,), (0,)), ((), ())), preferred_element_type=jnp.float32
    ).astype(jnp.bfloat16)


def near_kernel(send_cap, table_ref, lists_ref, counts_ref, own_ref, high_ref, low_ref, best_ref,
                other_code_ref, query_code_ref, key_ref, own_high, own_low):
    cap = lists_ref.shape[1]
    core = lax.axis_index("tiles").astype(jnp.int32)
    back, one, two = (table_ref[row : row + 1] for row in range(3))
    own = down_rows(jnp.where(core == 0, one, two))[:, :1]
    other = down_rows(jnp.where(core == 0, two, one))[:, :1]
    wide = down_rows(back)
    key_ref[...] = wide
    key = wide[:, :1]
    lists, counts = lists_ref[...], counts_ref[...]
    own_code = codes_of(lists, counts, core, own)
    query_code = across_lanes(codes_of(lists, counts, core, key))
    query_code_ref[...] = query_code
    other_code_ref[...] = jnp.broadcast_to(
        codes_of(lists, counts, 1 - core, other), other_code_ref.shape
    )
    turn = jnp.where(own == back, 1.0, 0.0).astype(jnp.bfloat16)
    split_rows(own_ref, own_high, own_low, send_cap)
    high, low = own_high[...], own_low[...]
    high_ref[...] = turned(high, turn)
    low_ref[...] = turned(low, turn)
    best_ref[...] = best_of(
        high, low, high_ref[...], low_ref[...], own_code, query_code, cap
    )


def far_kernel(send_cap, cap, high_ref, low_ref, best_ref, other_code_ref, query_code_ref,
               other_ref, out_ref):
    width, rows = high_ref.shape
    each = rows // send_cap
    chunks = width // LANES
    step = 2
    scores = jnp.zeros((rows, rows), jnp.float32)
    for begin in range(0, chunks, step):
        part = jnp.concatenate(
            [
                jnp.concatenate(
                    [
                        other_ref[pl.ds(rank * chunks + chunk, each, stride=send_cap * chunks), :]
                        for rank in range(send_cap)
                    ],
                    axis=0,
                )
                for chunk in range(begin, begin + step)
            ],
            axis=1,
        )
        high, rest = parts_of(part)
        low = rest.astype(jnp.bfloat16)
        span = slice(begin * LANES, (begin + step) * LANES)
        high_turned, low_turned = high_ref[span, :], low_ref[span, :]
        scores += (
            jnp.dot(high, high_turned, preferred_element_type=jnp.float32)
            + jnp.dot(high, low_turned, preferred_element_type=jnp.float32)
            + jnp.dot(low, high_turned, preferred_element_type=jnp.float32)
        )
    best = jnp.maximum(
        best_ref[...], masked_max(scores, other_code_ref[...], query_code_ref[...], cap)
    )
    lane = lax.broadcasted_iota(jnp.int32, (each, LANES), 1)
    out = jnp.zeros((each, LANES), jnp.float32)
    for rank in range(send_cap):
        column = jnp.broadcast_to(best[:, rank * each : (rank + 1) * each], (LANES, each)).T
        out = jnp.where(lane == rank, column, out)
    out_ref[...] = out


def pick_kernel(send_cap, slot_ref, key_ref, back_ref, out_ref):
    homes = back_ref.shape[0]
    docs = slot_ref.shape[1]
    slot, key, back = slot_ref[...], key_ref[...], back_ref[...]
    picked = jnp.zeros((homes, docs), jnp.float32)
    for rank in range(send_cap):
        value = jnp.broadcast_to(back[:, rank : rank + 1], (homes, docs))
        picked = jnp.where(slot == key[rank * homes : (rank + 1) * homes], value, picked)
    out_ref[...] = jnp.sum(picked, axis=0, keepdims=True)


def local(embeddings, cluster_of, row_lists, row_counts):
    n_docs = lax.axis_size("docs")
    n_tiles = lax.axis_size("tiles")
    doc_count, width = embeddings.shape
    send_cap = n_tiles * doc_count // n_docs
    cl_local = row_lists.shape[0]
    slots = n_docs * send_cap
    flat = (slots * width // LANES, LANES)
    vmem = pl.BlockSpec(memory_space=pltpu.VMEM)

    hbm = pl.BlockSpec(memory_space=pltpu.HBM)

    def in_hbm(array):
        return pltpu.with_memory_space_constraint(array, pltpu.HBM)

    order = return_order()
    firsts = [group_order(core) for core in range(n_tiles)]
    table = np.zeros((1 + 2 * n_tiles, slots), np.int32)
    for row, homes in enumerate([order] + firsts):
        table[row] = [home * send_cap + rank for rank in range(send_cap) for home in homes]
    for core, homes in enumerate(firsts):
        table[1 + n_tiles + core, homes] = range(n_docs)
    outgoing, slot, blocks, lists, counts = pl.pallas_call(
        functools.partial(prep_kernel, cl_local, send_cap),
        out_shape=(
            jax.ShapeDtypeStruct(flat, jnp.float32),
            jax.ShapeDtypeStruct((1, doc_count), jnp.int32),
            jax.ShapeDtypeStruct(table.shape, jnp.int32),
            jax.ShapeDtypeStruct(row_lists.shape, jnp.int32),
            jax.ShapeDtypeStruct((1, cl_local), jnp.int32),
        ),
        in_specs=[hbm] * 5,
        out_specs=(vmem,) * 5,
        scratch_shapes=[
            pltpu.VMEM((1, doc_count), jnp.int32),
            pltpu.VMEM((doc_count, width), jnp.float32),
            pltpu.SemaphoreType.DMA((5,)),
        ],
        compiler_params=PARAMS,
        name="prep",
    )(
        in_hbm(jnp.asarray(table)),
        in_hbm(cluster_of.reshape(1, doc_count)),
        in_hbm(row_lists),
        in_hbm(row_counts.reshape(1, cl_local)),
        in_hbm(embeddings),
    )

    def exchange(blocks, axis, groups):
        return lax.all_to_all(
            blocks, axis, split_axis=0, concat_axis=0, tiled=True, axis_index_groups=groups
        )

    groups = [[home * n_tiles + core for home in homes] for core, homes in enumerate(firsts)]
    own = exchange(outgoing.reshape(n_docs, -1, LANES), ("docs", "tiles"), groups)
    own = own.reshape(flat)
    other = lax.ppermute(own, "tiles", [(0, 1), (1, 0)])

    cap = row_lists.shape[1]
    turned = jax.ShapeDtypeStruct((width, slots), jnp.bfloat16)
    parts = [pltpu.VMEM((slots, width), jnp.bfloat16)] * 2
    *near, key = pl.pallas_call(
        functools.partial(near_kernel, send_cap),
        out_shape=(
            turned,
            turned,
            jax.ShapeDtypeStruct((1, slots), jnp.float32),
            jax.ShapeDtypeStruct((slots, slots), jnp.int32),
            jax.ShapeDtypeStruct((1, slots), jnp.int32),
            jax.ShapeDtypeStruct((slots, LANES), jnp.int32),
        ),
        in_specs=[vmem] * 4,
        out_specs=(vmem,) * 6,
        scratch_shapes=parts,
        compiler_params=PARAMS,
        name="near",
    )(blocks, lists, counts, own)
    best = pl.pallas_call(
        functools.partial(far_kernel, send_cap, cap),
        out_shape=jax.ShapeDtypeStruct((n_docs, LANES), jnp.float32),
        in_specs=[vmem] * 6,
        out_specs=vmem,
        compiler_params=PARAMS,
        name="far",
    )(*near, other)

    back = exchange(best.reshape(n_docs, 1, LANES), "docs", [order]).reshape(n_docs, LANES)
    picked = pl.pallas_call(
        functools.partial(pick_kernel, send_cap),
        out_shape=jax.ShapeDtypeStruct((1, doc_count), jnp.float32),
        in_specs=[vmem] * 3,
        out_specs=vmem,
        compiler_params=PARAMS,
        name="pick",
    )(slot, key, back)
    return picked.reshape(doc_count)


def solution(mesh):
    placed = (P(("docs", "tiles"), None), P(("docs", "tiles")), P("docs", None), P("docs"))
    return jax.shard_map(
        local, mesh=mesh, in_specs=placed, out_specs=P(("docs", "tiles")), check_vma=False
    )
```

```python
import functools

import jax
import jax.numpy as jnp
import numpy as np
from jax import lax
from jax.experimental import pallas as pl
from jax.experimental.pallas import tpu as pltpu
from jax.sharding import PartitionSpec as P

EPS = 1e-06
LANES = 128
GRID = (8, 4, 4)
PARAMS = pltpu.CompilerParams(vmem_limit_bytes=32 * 1024 * 1024)


def group_order(ahead):
    spots = [
        (z, x, y) for z in range(GRID[0]) for x in range(GRID[1]) for y in range(GRID[2])
    ]
    first = (GRID[0] // 2 + ahead, GRID[1] // 2, GRID[2] // 2)

    def distance(spot):
        gaps = [abs(at - start) for at, start in zip(spot, first)]
        return sum(min(gap, size - gap) for gap, size in zip(gaps, GRID))

    return sorted(
        range(len(spots)), key=lambda index: (distance(spots[index]) > 0, -distance(spots[index]))
    )


def return_order():
    count = GRID[0] * GRID[1] * GRID[2]
    bits = count.bit_length() - 1
    first = group_order(0)[0]
    return [
        first ^ sum((index >> bit & 1) << (bits - 1 - bit) for bit in range(bits))
        for index in range(count)
    ]


def parts_of(rows):
    high = rows.astype(jnp.bfloat16)
    rest = rows - high.astype(jnp.float32)
    return high, rest


def codes_of(lists, counts, half, key):
    cap = lists.shape[1]
    rows = key.shape[0]
    place = half * rows + key
    position = lax.broadcasted_iota(jnp.int32, (1, cap), 1)
    code = jnp.full((rows, cap), -1, jnp.int32)
    for cluster in range(lists.shape[0]):
        listed = jnp.where(position < counts[:, cluster : cluster + 1],
                           lists[cluster : cluster + 1, :], -1)
        code = jnp.where(listed == place, position + cluster * cap, code)
    return jnp.max(code, axis=1, keepdims=True)


def prep_kernel(cl_local, send_cap, table_hbm, cluster_hbm, lists_hbm, counts_hbm, rows_hbm,
                out_ref, slot_ref, table_ref, lists_ref, counts_ref,
                cluster_ref, rows_ref, sems):
    docs, width = rows_ref.shape
    slots = out_ref.shape[0] * LANES // width
    chunks = width // LANES
    copies = [
        pltpu.make_async_copy(source, target, sems.at[index])
        for index, (source, target) in enumerate(
            (
                (cluster_hbm, cluster_ref),
                (table_hbm, table_ref),
                (lists_hbm, lists_ref),
                (counts_hbm, counts_ref),
                (rows_hbm, rows_ref),
            )
        )
    ]
    for copy in copies:
        copy.start()
    for copy in copies[:2]:
        copy.wait()
    home = lax.shift_right_logical(cluster_ref[...], cl_local.bit_length() - 1)
    across = jnp.broadcast_to(home, (docs, docs))
    down = across.T
    sub = lax.broadcasted_iota(jnp.int32, (docs, docs), 0)
    lane = lax.broadcasted_iota(jnp.int32, (docs, docs), 1)
    before = jnp.where((across == down) & (sub < lane), 1, 0)
    rank = jnp.sum(before, axis=0, keepdims=True)
    slot_ref[...] = home * send_cap + rank
    homes = slots // send_cap
    core = lax.axis_index("tiles").astype(jnp.int32)
    blocks = jnp.where(core == 0, table_ref[3:4, :homes], table_ref[4:5, :homes])
    named = lax.broadcasted_iota(jnp.int32, (homes, docs), 0) == home
    blocks = jnp.broadcast_to(blocks.astype(jnp.float32), (8, homes))
    block = jnp.dot(
        blocks.astype(jnp.bfloat16),
        jnp.where(named, 1.0, 0.0).astype(jnp.bfloat16),
        preferred_element_type=jnp.float32,
    )[:1].astype(jnp.int32)
    place = lax.broadcasted_iota(jnp.int32, (slots, docs), 0)
    chosen = place == block * send_cap + rank
    chosen = jnp.where(chosen, 1.0, 0.0).astype(jnp.bfloat16)
    copies[-1].wait()
    rows = rows_ref[...]
    unit = rows * lax.rsqrt(jnp.sum(rows * rows, axis=1, keepdims=True) + EPS)
    high, rest = parts_of(unit)
    placed = jnp.dot(
        jnp.concatenate([chosen, chosen], axis=1),
        jnp.concatenate([high, rest.astype(jnp.bfloat16)], axis=0),
        preferred_element_type=jnp.float32,
    )
    for chunk in range(chunks):
        out_ref[pl.ds(chunk, slots, stride=chunks), :] = placed[
            :, chunk * LANES : (chunk + 1) * LANES
        ]
    for copy in copies[2:-1]:
        copy.wait()


def split_rows(rows_ref, high_ref, low_ref, send_cap):
    count, width = high_ref.shape
    chunks = width // LANES
    each = count // send_cap
    for rank in range(send_cap):
        for chunk in range(chunks):
            part = rows_ref[pl.ds(rank * chunks + chunk, each, stride=send_cap * chunks), :]
            high, rest = parts_of(part)
            cols = slice(chunk * LANES, (chunk + 1) * LANES)
            high_ref[rank * each : (rank + 1) * each, cols] = high
            low_ref[rank * each : (rank + 1) * each, cols] = rest.astype(jnp.bfloat16)


def across_lanes(column):
    wide = jnp.broadcast_to(column, (column.shape[0], LANES))
    return wide.T[:1, :]


def masked_max(scores, key_code, query_code, cap):
    first = query_code // cap * cap
    allowed = (key_code < query_code) & (key_code >= first)
    return jnp.max(jnp.where(allowed, scores, -1.0), axis=0, keepdims=True)


def best_of(key_high, key_low, high_turned, low_turned, key_code, query_code, cap):
    def dot(keys, queries):
        return jnp.dot(keys, queries, preferred_element_type=jnp.float32)

    scores = dot(key_high, high_turned) + (
        dot(key_high, low_turned) + dot(key_low, high_turned)
    )
    return masked_max(scores, key_code, query_code, cap)


def down_rows(row):
    return jnp.broadcast_to(row, (LANES, row.shape[1])).T


def turned(rows, turn):
    return lax.dot_general(
        rows, turn, (((0,), (0,)), ((), ())), preferred_element_type=jnp.float32
    ).astype(jnp.bfloat16)


def near_kernel(send_cap, table_ref, lists_ref, counts_ref, own_ref, high_ref, low_ref, best_ref,
                other_code_ref, query_code_ref, key_ref, own_high, own_low):
    cap = lists_ref.shape[1]
    core = lax.axis_index("tiles").astype(jnp.int32)
    back, one, two = (table_ref[row : row + 1] for row in range(3))
    own = down_rows(jnp.where(core == 0, one, two))[:, :1]
    other = down_rows(jnp.where(core == 0, two, one))[:, :1]
    wide = down_rows(back)
    key_ref[...] = wide
    key = wide[:, :1]
    lists, counts = lists_ref[...], counts_ref[...]
    own_code = codes_of(lists, counts, core, own)
    query_code = across_lanes(codes_of(lists, counts, core, key))
    query_code_ref[...] = query_code
    other_code_ref[...] = codes_of(lists, counts, 1 - core, other)
    turn = jnp.where(own == back, 1.0, 0.0).astype(jnp.bfloat16)
    split_rows(own_ref, own_high, own_low, send_cap)
    high, low = own_high[...], own_low[...]
    high_ref[...] = turned(high, turn)
    low_ref[...] = turned(low, turn)
    best_ref[...] = best_of(
        high, low, high_ref[...], low_ref[...], own_code, query_code, cap
    )


def far_kernel(send_cap, cap, high_ref, low_ref, best_ref, other_code_ref, query_code_ref,
               other_ref, out_ref):
    width, rows = high_ref.shape
    each = rows // send_cap
    chunks = width // LANES
    step = 2
    scores = jnp.zeros((rows, rows), jnp.float32)
    for begin in range(0, chunks, step):
        part = jnp.concatenate(
            [
                jnp.concatenate(
                    [
                        other_ref[pl.ds(rank * chunks + chunk, each, stride=send_cap * chunks), :]
                        for rank in range(send_cap)
                    ],
                    axis=0,
                )
                for chunk in range(begin, begin + step)
            ],
            axis=1,
        )
        high, rest = parts_of(part)
        low = rest.astype(jnp.bfloat16)
        span = slice(begin * LANES, (begin + step) * LANES)
        high_turned, low_turned = high_ref[span, :], low_ref[span, :]
        scores += (
            jnp.dot(high, high_turned, preferred_element_type=jnp.float32)
            + jnp.dot(high, low_turned, preferred_element_type=jnp.float32)
            + jnp.dot(low, high_turned, preferred_element_type=jnp.float32)
        )
    best = jnp.maximum(
        best_ref[...], masked_max(scores, other_code_ref[...], query_code_ref[...], cap)
    )
    lane = lax.broadcasted_iota(jnp.int32, (each, LANES), 1)
    out = jnp.zeros((each, LANES), jnp.float32)
    for rank in range(send_cap):
        column = jnp.broadcast_to(best[:, rank * each : (rank + 1) * each], (LANES, each)).T
        out = jnp.where(lane == rank, column, out)
    out_ref[...] = out


def pick_kernel(send_cap, slot_ref, key_ref, back_ref, out_ref):
    homes = back_ref.shape[0]
    docs = slot_ref.shape[1]
    slot, key, back = slot_ref[...], key_ref[...], back_ref[...]
    picked = jnp.zeros((homes, docs), jnp.float32)
    for rank in range(send_cap):
        value = jnp.broadcast_to(back[:, rank : rank + 1], (homes, docs))
        picked = jnp.where(slot == key[rank * homes : (rank + 1) * homes], value, picked)
    out_ref[...] = jnp.sum(picked, axis=0, keepdims=True)


def local(embeddings, cluster_of, row_lists, row_counts):
    n_docs = lax.axis_size("docs")
    n_tiles = lax.axis_size("tiles")
    doc_count, width = embeddings.shape
    send_cap = n_tiles * doc_count // n_docs
    cl_local = row_lists.shape[0]
    slots = n_docs * send_cap
    flat = (slots * width // LANES, LANES)
    vmem = pl.BlockSpec(memory_space=pltpu.VMEM)

    hbm = pl.BlockSpec(memory_space=pltpu.HBM)

    def in_hbm(array):
        return pltpu.with_memory_space_constraint(array, pltpu.HBM)

    order = return_order()
    firsts = [group_order(core) for core in range(n_tiles)]
    table = np.zeros((1 + 2 * n_tiles, slots), np.int32)
    for row, homes in enumerate([order] + firsts):
        table[row] = [home * send_cap + rank for rank in range(send_cap) for home in homes]
    for core, homes in enumerate(firsts):
        table[1 + n_tiles + core, homes] = range(n_docs)
    outgoing, slot, blocks, lists, counts = pl.pallas_call(
        functools.partial(prep_kernel, cl_local, send_cap),
        out_shape=(
            jax.ShapeDtypeStruct(flat, jnp.float32),
            jax.ShapeDtypeStruct((1, doc_count), jnp.int32),
            jax.ShapeDtypeStruct(table.shape, jnp.int32),
            jax.ShapeDtypeStruct(row_lists.shape, jnp.int32),
            jax.ShapeDtypeStruct((1, cl_local), jnp.int32),
        ),
        in_specs=[hbm] * 5,
        out_specs=(vmem,) * 5,
        scratch_shapes=[
            pltpu.VMEM((1, doc_count), jnp.int32),
            pltpu.VMEM((doc_count, width), jnp.float32),
            pltpu.SemaphoreType.DMA((5,)),
        ],
        compiler_params=PARAMS,
        name="prep",
    )(
        in_hbm(jnp.asarray(table)),
        in_hbm(cluster_of.reshape(1, doc_count)),
        in_hbm(row_lists),
        in_hbm(row_counts.reshape(1, cl_local)),
        in_hbm(embeddings),
    )

    def exchange(blocks, axis, groups):
        return lax.all_to_all(
            blocks, axis, split_axis=0, concat_axis=0, tiled=True, axis_index_groups=groups
        )

    groups = [[home * n_tiles + core for home in homes] for core, homes in enumerate(firsts)]
    own = exchange(outgoing.reshape(n_docs, -1, LANES), ("docs", "tiles"), groups)
    own = own.reshape(flat)
    other = lax.ppermute(own, "tiles", [(0, 1), (1, 0)])

    cap = row_lists.shape[1]
    turned = jax.ShapeDtypeStruct((width, slots), jnp.bfloat16)
    parts = [pltpu.VMEM((slots, width), jnp.bfloat16)] * 2
    *near, key = pl.pallas_call(
        functools.partial(near_kernel, send_cap),
        out_shape=(
            turned,
            turned,
            jax.ShapeDtypeStruct((1, slots), jnp.float32),
            jax.ShapeDtypeStruct((slots, 1), jnp.int32),
            jax.ShapeDtypeStruct((1, slots), jnp.int32),
            jax.ShapeDtypeStruct((slots, LANES), jnp.int32),
        ),
        in_specs=[vmem] * 4,
        out_specs=(vmem,) * 6,
        scratch_shapes=parts,
        compiler_params=PARAMS,
        name="near",
    )(blocks, lists, counts, own)
    best = pl.pallas_call(
        functools.partial(far_kernel, send_cap, cap),
        out_shape=jax.ShapeDtypeStruct((n_docs, LANES), jnp.float32),
        in_specs=[vmem] * 6,
        out_specs=vmem,
        compiler_params=PARAMS,
        name="far",
    )(*near, other)

    back = exchange(best.reshape(n_docs, 1, LANES), "docs", [order]).reshape(n_docs, LANES)
    picked = pl.pallas_call(
        functools.partial(pick_kernel, send_cap),
        out_shape=jax.ShapeDtypeStruct((1, doc_count), jnp.float32),
        in_specs=[vmem] * 3,
        out_specs=vmem,
        compiler_params=PARAMS,
        name="pick",
    )(slot, key, back)
    return picked.reshape(doc_count)


def solution(mesh):
    placed = (P(("docs", "tiles"), None), P(("docs", "tiles")), P("docs", None), P("docs"))
    return jax.shard_map(
        local, mesh=mesh, in_specs=placed, out_specs=P(("docs", "tiles")), check_vma=False
    )
```
